128 devices in a mesh: fsdp: 16 (over x, y_hi, core), dp: 8 (over y_lo, z).
Axes of the slice: x: 4, y: 4 (y_hi: 2, y_lo: 2; y = y_hi * 2 + y_lo), z: 4, core: 2. Of those that a mesh axis runs over, the one named last changes fastest.
Arguments:
- codes: int32 [9, 16384], P(None, ('fsdp', 'dp')), may hold values from 0 to 1023
- lengths: int32 [1024], P(('fsdp', 'dp')), may hold values from 1 to 16
- owner: int32 [1024, 1], P(('fsdp', 'dp')), may hold values from 0 to 7; in each aligned block of 8 rows (0 to 7, 8 to 15, ...) at most 2 rows name the same one
- codebook: float32 [9, 1024, 1024], P(None, 'fsdp'), may hold values from -5 to 5
- latent_projection_weight: float32 [1024, 1536], P('fsdp'), may hold values from -0.1875 to 0.1875
- snake_upsample_first: float32 [1536], replicated, may hold values from 0.5 to 4
- upsample_weight_first: float32 [1536, 1536], P('fsdp'), may hold values from -0.15625 to 0.15625
- snake_residual_first: float32 [768], replicated, may hold values from 0.5 to 4
- dilated_weight_first: float32 [7, 768, 768], P(None, 'fsdp'), may hold values from -0.078125 to 0.078125
- mixing_weight_first: float32 [768, 768], P('fsdp'), may hold values from -0.21875 to 0.21875
- snake_upsample_second: float32 [768], replicated, may hold values from 0.5 to 4
- upsample_weight_second: float32 [768, 768], P('fsdp'), may hold values from -0.21875 to 0.21875
- snake_residual_second: float32 [384], replicated, may hold values from 0.5 to 4
- dilated_weight_second: float32 [7, 384, 384], P(None, 'fsdp'), may hold values from -0.125 to 0.125
- mixing_weight_second: float32 [384, 384], P('fsdp'), may hold values from -0.3125 to 0.3125
Outputs:
- decoded: bfloat16 [131072, 384], P(('fsdp', 'dp'))
The draws below stay inside these ranges and needn't reach their ends.
Inputs may be any that keep to these rules, and one draw needn't show every extreme that they name: Among the slabs of one device no owner appears more than 2 times, and some device sends exactly 2 slabs to one owner.
All inputs are finite; a program needn't handle non-finite values.
Results may differ from the reference program's by a relative error of at most 0.015.
Values may be sent and summed in bfloat16 or wider, within the bound.
A program may use at most 320 MiB of HBM per device.

```python
import math
import jax
import jax.numpy as jnp
import numpy as np

CD = 1024
CODES = 1024
C0 = 1536
FIRST_CHANNELS = 768
SECOND_CHANNELS = 384
LEVELS = 9
SLAB = 16
FIRST_DILATION = 3
SECOND_DILATION = 9
SLABS = 8
MOST = 2
SLAB_TOTAL = 1024
OUT_SLOTS = 2048
N_FSDP = 16
N_DP = 8


def with_ends(entries, own_key, low, high):
    longest = entries.shape.index(max(entries.shape))
    spots = []
    for shift in (0, 1):
        where = [jax.random.randint(jax.random.fold_in(own_key, axis), (), 0, length) for axis, length in enumerate(entries.shape)]
        where[longest] = (where[longest] + shift) % entries.shape[longest]
        spots.append(tuple(where))
    return entries.at[spots[0]].set(low).at[spots[1]].set(high)


def block_scale(stream_key, shape, pieces, smallest, high):
    level = 1.0
    for dim, blocks in pieces:
        heights = jax.random.uniform(jax.random.fold_in(jax.random.fold_in(stream_key, 6), dim), (blocks,), jnp.float32, smallest / len(pieces), high / len(pieces))
        level = level * jnp.repeat(jnp.exp(heights), shape[dim] // blocks).reshape((-1,) + (1,) * (len(shape) - 1 - dim))
    return level


def shared_out(rng, own, number, rows, number_of, top, limit, skew):
    ranking = jax.random.permutation(rng, number_of)
    crowded, common = shares(number_of, rows * top, limit, skew, True), shares(number_of, rows * top, limit, skew, False)
    places = jnp.arange(number_of)

    def named(tallies, turn):
        used = int((tallies > 0).sum())
        fixed = max(1, used // 4)
        passed = fixed + (places - fixed + turn * (used - fixed)) % max(1, number_of - fixed)
        return jnp.zeros((number_of,), jnp.int32).at[ranking[jnp.where(places < fixed, places, passed)]].set(jnp.asarray(tallies, jnp.int32))

    tallies = jnp.where(number % 4 == 0, named(crowded, number // 4), named(common, number - number // 4 - 1))
    mixed = jax.random.permutation(jax.random.fold_in(own, 3), number_of)
    giver, taker = mixed[0:number_of // 2 * 2:2], mixed[1:number_of // 2 * 2:2]
    slack = jnp.minimum(tallies[giver] - 1, limit - tallies[taker]) // 2
    slack = jnp.where((giver == ranking[0]) | (taker == ranking[0]) | (tallies[taker] == 0), 0, jnp.maximum(slack, 0))
    passed = jax.random.randint(jax.random.fold_in(own, 4), (number_of // 2,), 0, 1 << 20) % (slack + 1)
    tallies = tallies.at[giver].add(-passed).at[taker].add(passed)
    members = jnp.searchsorted(jnp.cumsum(tallies), jnp.arange(rows * top), side="right").astype(jnp.int32)
    listing = members.reshape(top, rows).T
    listing = listing[jax.random.permutation(jax.random.fold_in(own, 1), rows)]
    turn = jax.random.randint(jax.random.fold_in(own, 2), (rows, 1), 0, top)
    return jnp.take_along_axis(listing, (jnp.arange(top)[None, :] + turn) % top, axis=1)


def shares(count, total, bound, slope, full):
    weights = [(1 << 20) // math.isqrt(rank ** slope) + 1 for rank in range(1, count + 1)]
    largest = bound if full else min(bound, max(-(-total // count), total * weights[0] // sum(weights)))
    least = 1 if total - largest >= count - 1 else 0
    counts, rest = [largest] + [least] * (count - 1), total - largest - least * (count - 1)
    while rest > 0:
        free = [i for i in range(1, count) if counts[i] < largest] or [i for i in range(1, count) if counts[i] < bound]
        mass, budget = sum([weights[i] for i in free]), rest
        for i in free:
            addition = min(bound - counts[i], max(1, budget * weights[i] // mass), rest)
            counts[i] = counts[i] + addition
            rest = rest - addition
    return np.array(counts)


def gaussian(rng, extent, deviation, most, pieces=(), kind=jnp.bfloat16):
    loudness = block_scale(rng, extent, pieces, -0.22, 0.18) if pieces else 1.0
    entries = jax.random.normal(rng, extent, jnp.float32) * deviation * loudness
    return jnp.minimum(jnp.maximum(entries, -most), most).astype(kind)


def setup_inputs(seed: int = 0) -> dict:
    arg_keys = jax.random.split(jax.random.key(seed), 16)
    codes = with_ends(jax.random.randint(arg_keys[0], (LEVELS, SLAB_TOTAL * SLAB), 0, CODES), jax.random.fold_in(arg_keys[0], 1), 0, CODES - 1).astype(jnp.int32)
    lengths = with_ends(jax.random.randint(arg_keys[1], (SLAB_TOTAL,), 1, SLAB + 1), jax.random.fold_in(arg_keys[1], 1), 1, SLAB).astype(jnp.int32)
    owner_keys = jax.random.split(jax.random.fold_in(arg_keys[2], 1), SLAB_TOTAL // SLABS)
    owner_turns = jax.random.permutation(jax.random.fold_in(arg_keys[2], 3), SLAB_TOTAL // SLABS)
    owner = jax.vmap(lambda own, number: shared_out(jax.random.fold_in(arg_keys[2], 2), own, number, SLABS, N_DP, 1, MOST, 2))(owner_keys, owner_turns).reshape((SLAB_TOTAL, 1))
    codebook = gaussian(arg_keys[3], (LEVELS, CODES, CD), 0.33, 5.0, ((1, 16),), jnp.float32)
    latent_projection_weight = gaussian(arg_keys[4], (CD, C0), CD ** -0.5, 0.1875, ((0, 16),), jnp.float32)
    snake_upsample_first = jnp.clip(jnp.exp(jax.random.uniform(arg_keys[5], (C0,), jnp.float32, math.log(0.5), math.log(4.0))), 0.5, 4.0)
    upsample_weight_first = gaussian(arg_keys[6], (C0, 2 * FIRST_CHANNELS), C0 ** -0.5, 0.15625, ((0, 16),), jnp.float32)
    snake_residual_first = jnp.clip(jnp.exp(jax.random.uniform(arg_keys[7], (FIRST_CHANNELS,), jnp.float32, math.log(0.5), math.log(4.0))), 0.5, 4.0)
    dilated_weight_first = gaussian(arg_keys[8], (7, FIRST_CHANNELS, FIRST_CHANNELS), (7 * FIRST_CHANNELS) ** -0.5, 0.078125, ((1, 16),), jnp.float32)
    mixing_weight_first = gaussian(arg_keys[9], (FIRST_CHANNELS, FIRST_CHANNELS), FIRST_CHANNELS ** -0.5, 0.21875, ((0, 16),), jnp.float32)
    snake_upsample_second = jnp.clip(jnp.exp(jax.random.uniform(arg_keys[10], (FIRST_CHANNELS,), jnp.float32, math.log(0.5), math.log(4.0))), 0.5, 4.0)
    upsample_weight_second = gaussian(arg_keys[11], (FIRST_CHANNELS, 2 * SECOND_CHANNELS), FIRST_CHANNELS ** -0.5, 0.21875, ((0, 16),), jnp.float32)
    snake_residual_second = jnp.clip(jnp.exp(jax.random.uniform(arg_keys[12], (SECOND_CHANNELS,), jnp.float32, math.log(0.5), math.log(4.0))), 0.5, 4.0)
    dilated_weight_second = gaussian(arg_keys[13], (7, SECOND_CHANNELS, SECOND_CHANNELS), (7 * SECOND_CHANNELS) ** -0.5, 0.125, ((1, 16),), jnp.float32)
    mixing_weight_second = gaussian(arg_keys[14], (SECOND_CHANNELS, SECOND_CHANNELS), SECOND_CHANNELS ** -0.5, 0.3125, ((0, 16),), jnp.float32)
    return dict(codes=codes, lengths=lengths, owner=owner, codebook=codebook, latent_projection_weight=latent_projection_weight, snake_upsample_first=snake_upsample_first, upsample_weight_first=upsample_weight_first, snake_residual_first=snake_residual_first, dilated_weight_first=dilated_weight_first, mixing_weight_first=mixing_weight_first, snake_upsample_second=snake_upsample_second, upsample_weight_second=upsample_weight_second, snake_residual_second=snake_residual_second, dilated_weight_second=dilated_weight_second, mixing_weight_second=mixing_weight_second)


def snake(value, snake_frequency):
    return value + jnp.sin(snake_frequency * value) ** 2 / snake_frequency


def matmul(left, weight):
    shape = left.shape
    flat = left.reshape(-1, shape[-1])
    return jnp.dot(flat, weight, preferred_element_type=jnp.float32).reshape(shape[:-1] + (weight.shape[1],))


def dilated_output(values, weight, dilation_step):
    frames = values.shape[1]
    half = 3 * dilation_step
    padded = jnp.pad(values, ((0, 0), (half, half), (0, 0)))
    total = jnp.zeros(values.shape[:2] + (weight.shape[2],), jnp.float32)
    for tap in range(7):
        total = total + matmul(padded[:, tap * dilation_step:tap * dilation_step + frames], weight[tap])
    return total


def residual_stack_unit(upper_bound, snake_frequency, dilated_weight, mixing_weight, dilation_step):
    active_frames = snake(upper_bound, snake_frequency).astype(jnp.bfloat16)
    apply_convolution = dilated_output(active_frames, dilated_weight, dilation_step)
    second = snake(apply_convolution, snake_frequency).astype(jnp.bfloat16)
    return upper_bound + matmul(second, mixing_weight)


def reference(codes, lengths, owner, codebook, latent_projection_weight, snake_upsample_first, upsample_weight_first, snake_residual_first, dilated_weight_first, mixing_weight_first, snake_upsample_second, upsample_weight_second, snake_residual_second, dilated_weight_second, mixing_weight_second):
    brain_float = jnp.bfloat16
    table = codebook.astype(brain_float)
    frames_all = codes.shape[1]
    latent = jnp.zeros((frames_all, CD), jnp.float32)
    for level in range(LEVELS):
        latent = latent + jnp.take(table[level], codes[level], axis=0).astype(jnp.float32)
    place = jnp.arange(frames_all, dtype=jnp.int32)
    keep = (place % SLAB) < jnp.repeat(lengths, SLAB)
    latent = jnp.where(keep[:, None], latent.astype(brain_float), jnp.zeros((), brain_float))
    slabs = latent.reshape(SLAB_TOTAL, SLAB, CD)
    start = matmul(slabs, latent_projection_weight.astype(brain_float))
    lifted_one = snake(start, snake_upsample_first).astype(brain_float)
    upsampled_first = matmul(lifted_one, upsample_weight_first.astype(brain_float)).reshape(SLAB_TOTAL, 2 * SLAB, FIRST_CHANNELS)
    decoder_block_first = residual_stack_unit(upsampled_first, snake_residual_first, dilated_weight_first.astype(brain_float), mixing_weight_first.astype(brain_float), FIRST_DILATION)
    lifted_two = snake(decoder_block_first, snake_upsample_second).astype(brain_float)
    upsampled_second = matmul(lifted_two, upsample_weight_second.astype(brain_float)).reshape(SLAB_TOTAL, 4 * SLAB, SECOND_CHANNELS)
    decoder_block_second = residual_stack_unit(upsampled_second, snake_residual_second, dilated_weight_second.astype(brain_float), mixing_weight_second.astype(brain_float), SECOND_DILATION).astype(brain_float)
    groups = N_FSDP * N_DP
    dest = owner[:, 0].reshape(groups, SLABS)
    order = jnp.arange(SLABS, dtype=jnp.int32)
    earlier = (dest[:, None, :] == dest[:, :, None]) & (order[None, None, :] < order[None, :, None])
    rank = jnp.sum(earlier.astype(jnp.int32), axis=2)
    device = jnp.arange(groups, dtype=jnp.int32)[:, None]
    fpart = device // N_DP
    dpart = device % N_DP
    slot = ((fpart * N_DP + dest) * N_DP + dpart) * MOST + rank
    result = jnp.zeros((OUT_SLOTS, 4 * SLAB, SECOND_CHANNELS), brain_float)
    result = result.at[slot.reshape(-1).astype(jnp.int32)].set(decoder_block_second)
    return result.reshape(OUT_SLOTS * 4 * SLAB, SECOND_CHANNELS)
```

```python
import jax
import jax.numpy as jnp
from jax import lax
from jax.experimental import pallas as pl
from jax.experimental.pallas import tpu as pltpu
from jax.sharding import PartitionSpec as P

SLAB = 16
MOST = 2
BF = jnp.bfloat16
F32 = jnp.float32
POLY = (
    9.869604311819561,
    -32.46967117891694,
    42.72719645855932,
    -30.101466599015037,
    13.05010051862992,
    -3.3565928630444257,
)
INV_PI = 0.3183098861837907
PAD1 = 8
PAD2 = 26


def snake(value, freq):
    turns = value * (freq * INV_PI)
    frac = turns - jnp.round(turns)
    u = frac * frac
    poly = jnp.full_like(u, POLY[-1])
    for coef in POLY[-2::-1]:
        poly = poly * u + coef
    return value + (poly * u) * (1.0 / freq)


def dot(left, right):
    return jnp.dot(left, right, preferred_element_type=F32)


class Links:
    def __init__(self, send_sems, recv_sems):
        self.send_sems, self.recv_sems, self.used, self.sent = send_sems, recv_sems, 0, []

    def new(self):
        self.used += 1
        return self.used - 1

    def copy(self, src, dst, dev, number):
        return pltpu.make_async_remote_copy(
            src_ref=src,
            dst_ref=dst,
            send_sem=self.send_sems.at[number],
            recv_sem=self.recv_sems.at[number],
            device_id=dev,
            device_id_type=pl.DeviceIdType.MESH,
        )

    def send(self, src, dev, number, dst=None):
        copy = self.copy(src, src if dst is None else dst, dev, number)
        copy.start()
        self.sent.append(copy)

    def wait(self, region, dev, number):
        self.copy(region, region, dev, number).wait_recv()


def kernel(
    codes_ref, src_ref, cb_hbm, w0_hbm, w1_hbm, w23_hbm, w4_hbm, w56_hbm, a0_ref, a1_ref, a2_ref, a3_ref,
    out_ref,
    codes_all, cbf, w0f, w1f, w23f, w4f, s56, table, onehot,
    fwd_out, fwd_in, far_out, far_in, sum_out, sum_in, keep, ypart_out, ypart_in,
    w0b, w1b, w23b, w4b, w56b,
    lat, lift1, up1, act_a1, act_b1, acc1, sec1, lift2, up2, act_a2, act_b2, sec2, block2, outbuf,
    send_sems, recv_sems, local_sems,
):
    f = lax.axis_index("fsdp")
    d = lax.axis_index("dp")
    x, yh, c = lax.div(f, 4), lax.rem(lax.div(f, 2), 2), lax.rem(f, 2)
    yl, z = lax.div(d, 4), lax.rem(d, 4)
    g = x * 2 + yh

    def dev(x_, yh_, yl_, z_, c_):
        return {"fsdp": (x_ * 2 + yh_) * 2 + c_, "dp": yl_ * 4 + z_}

    def plus(value, step):
        return lax.rem(value + step, 4)

    xp, xm, x2 = plus(x, 1), plus(x, 3), plus(x, 2)
    zp, zm, z2 = plus(z, 1), plus(z, 3), plus(z, 2)
    xs, xr = plus(x, 1 + 2 * c), plus(x, 3 + 2 * c)
    oyh = 1 - yh

    def at_x(xt):
        return dev(xt, yh, yl, z, c)

    def at_z(zt):
        return dev(x, yh, yl, zt, c)

    at_y = dev(x, oyh, 1 - yl, z, c)
    sib = dev(x, yh, yl, z, 1 - c)
    links = Links(send_sems, recv_sems)
    local_count = [0]

    def load(src, dst):
        copy = pltpu.make_async_copy(src, dst, local_sems.at[local_count[0]])
        local_count[0] += 1
        copy.start()
        return copy

    zcols = pl.ds(pl.multiple_of(z * 384, 384), 384)
    ld_cb = load(cb_hbm, cbf)
    ld_w1 = load(w1_hbm.at[:, zcols], w1f)
    ld_w23 = load(w23_hbm.at[pl.ds(2 * z, 2)], w23f)
    ld_w0 = load(w0_hbm, w0f)
    ld_w4 = load(w4_hbm, w4f)
    own24 = pl.ds(pl.multiple_of(c * 24, 8), 24)
    ld_w56 = load(w56_hbm.at[pl.ds(4 * c, 4)], s56.at[:, own24])
    codes_all[x, yh] = codes_ref[...]

    mates = []
    for step in range(4):
        if step:
            mates.append(at_x(plus(x, step)))
        mates.append(dev(plus(x, step), oyh, 1 - yl, z, c))
    owners = [lax.rem(d + step, 8) for step in range(1, 8)]
    barrier = pltpu.get_barrier_semaphore()
    peers = mates + [sib] + [{"fsdp": f, "dp": o} for o in owners]
    for peer in peers:
        pl.semaphore_signal(barrier, inc=1, device_id=peer, device_id_type=pl.DeviceIdType.MESH)
    pl.semaphore_wait(barrier, len(peers))

    code_ids = [links.new() for _ in mates]
    for number, mate in zip(code_ids, mates):
        links.send(codes_all.at[x, yh], mate, number)
    id_56 = links.new()
    links.send(w56_hbm.at[pl.ds(4 * (1 - c), 4)], sib, id_56, dst=s56.at[:, own24])

    ld_cb.wait()
    own64 = pl.ds(pl.multiple_of(c * 64, 64), 64)
    oth64 = pl.ds(pl.multiple_of((1 - c) * 64, 64), 64)
    for level in range(9):
        table[level, own64, :] = cbf[level].astype(BF)
    id_table = links.new()
    links.send(table.at[:, own64], sib, id_table)

    class Quarter:
        def __init__(self, block, row, full, half):
            self.block, self.row, self.full, self.half = block, row, full, half
            self.ids = [links.new() for _ in range(12)]

        def start(self):
            for number, xt in zip(self.ids[:3], (xp, xm, x2)):
                links.send(self.block(z, x, yh), at_x(xt), number)

        def to_y(self):
            for number, xt in zip(self.ids[:3], (xm, xp, x2)):
                links.wait(self.block(z, xt, yh), at_x(xt), number)
            links.send(self.row(z, yh), at_y, self.ids[3])

        def to_z(self):
            links.wait(self.row(z, oyh), at_y, self.ids[3])
            links.send(self.full(z), at_z(zp), self.ids[4])
            links.send(self.full(z), at_z(zm), self.ids[5])
            links.send(self.full(z), sib, self.ids[8])

        def pass_z(self):
            links.wait(self.full(zm), at_z(zm), self.ids[4])
            links.send(self.half(zm, 0), at_z(zp), self.ids[6])
            links.wait(self.full(zp), at_z(zp), self.ids[5])
            links.send(self.half(zp, 1), at_z(zm), self.ids[7])
            links.send(self.full(zm), sib, self.ids[9])
            links.send(self.full(zp), sib, self.ids[10])

        def finish(self):
            links.wait(self.half(z2, 0), at_z(zm), self.ids[6])
            links.wait(self.half(z2, 1), at_z(zp), self.ids[7])
            links.send(self.full(z2), sib, self.ids[11])

        def done(self):
            for number in self.ids[8:]:
                links.wait(self.full(z), sib, number)

    class Plain:
        def __init__(self, block, pair):
            self.block, self.pair = block, pair
            self.ids = [links.new() for _ in range(9)]

        def start(self):
            links.send(self.block(x, yh), at_y, self.ids[0])

        def to_x(self):
            links.wait(self.block(x, oyh), at_y, self.ids[0])
            links.send(self.pair(x), at_x(xp), self.ids[1])
            links.send(self.pair(x), at_x(xm), self.ids[2])
            links.send(self.pair(x), sib, self.ids[5])

        def pass_x(self):
            links.wait(self.pair(xm), at_x(xm), self.ids[1])
            links.send(self.block(xm, 0), at_x(xp), self.ids[3])
            links.wait(self.pair(xp), at_x(xp), self.ids[2])
            links.send(self.block(xp, 1), at_x(xm), self.ids[4])
            links.send(self.pair(xm), sib, self.ids[6])
            links.send(self.pair(xp), sib, self.ids[7])

        def finish(self):
            links.wait(self.block(x2, 0), at_x(xm), self.ids[3])
            links.wait(self.block(x2, 1), at_x(xp), self.ids[4])
            links.send(self.pair(x2), sib, self.ids[8])

        def done(self):
            for number in self.ids[5:]:
                links.wait(self.pair(x), sib, number)

    def columns(zt):
        return pl.ds(pl.multiple_of(zt * 384, 384), 384)

    q1 = Quarter(
        lambda zt, xt, yt: w1b.at[xt, yt, c, :, columns(zt)],
        lambda zt, yt: w1b.at[:, yt, c, :, columns(zt)],
        lambda zt: w1b.at[:, :, c, :, columns(zt)],
        lambda zt, h: w1b.at[:, h, c, :, columns(zt)],
    )

    def tap_quarter(odd):
        return Quarter(
            lambda zt, xt, yt: w23b.at[2 * zt + odd, xt, yt, c],
            lambda zt, yt: w23b.at[2 * zt + odd, :, yt, c],
            lambda zt: w23b.at[2 * zt + odd, :, :, c],
            lambda zt, h: w23b.at[2 * zt + odd, :, h, c],
        )

    qa, qb = tap_quarter(0), tap_quarter(1)
    p0 = Plain(lambda xt, yt: w0b.at[xt, yt, c], lambda xt: w0b.at[xt, :, c])
    p4 = Plain(lambda xt, yt: w4b.at[xt, yt, c], lambda xt: w4b.at[xt, :, c])
    p56 = Plain(lambda xt, yt: w56b.at[c, :, xt, yt], lambda xt: w56b.at[c, :, xt])

    ld_w1.wait()
    w1b[x, yh, c, :, zcols] = w1f[...].astype(BF)
    q1.start()
    ld_w0.wait()
    w0b[x, yh, c] = w0f[...].astype(BF)
    p0.start()
    ld_w23.wait()
    w23b[2 * z, x, yh, c] = w23f[0].astype(BF)
    qa.start()
    w23b[2 * z + 1, x, yh, c] = w23f[1].astype(BF)
    qb.start()
    ld_w4.wait()
    w4b[x, yh, c] = w4f[...].astype(BF)
    p4.start()
    ld_w56.wait()
    links.wait(s56.at[:, own24], sib, id_56)
    for tap in range(4):
        w56b[c, tap, x, yh] = s56[tap].astype(BF)
    p56.start()

    for number, mate in zip(code_ids, mates):
        links.wait(codes_all.at[x, yh], mate, number)
    links.wait(table.at[:, oth64], sib, id_table)

    def partial(xt, put):
        place = lax.broadcasted_iota(jnp.int32, (128, 128), 0) + g * 128
        for yt in range(2):
            codes = codes_all[xt, yt]
            for level in range(9):
                hit = codes[level : level + 1, :] == place
                onehot[pl.ds(level * 128, 128), pl.ds(yt * 128, 128)] = jnp.where(hit, 1.0, 0.0).astype(BF)

        def tile(n, carry):
            cols = pl.ds(pl.multiple_of(n * 256, 256), 256)
            rows = table[:, :, cols].reshape(1152, 256)
            total = lax.dot_general(onehot[...], rows, (((0,), (0,)), ((), ())), preferred_element_type=F32)
            put(cols, total)
            return carry

        lax.fori_loop(0, 4, tile, 0)

    def into(ref):
        def put(cols, total):
            ref[:, cols] = total.astype(ref.dtype)

        return put

    id_fwd, id_far, id_sum, id_y = (links.new() for _ in range(4))
    partial(x2, into(fwd_out))
    links.send(fwd_out, at_x(xs), id_fwd, dst=fwd_in)
    q1.to_y()
    p0.to_x()
    partial(xr, into(far_out))
    links.send(far_out, at_x(xr), id_far, dst=far_in)
    qa.to_y()
    partial(xs, into(keep))
    links.wait(fwd_in, at_x(xr), id_fwd)
    sum_out[...] = (keep[...] + fwd_in[...].astype(F32)).astype(BF)
    links.send(sum_out, at_x(xs), id_sum, dst=sum_in)
    q1.to_z()
    qb.to_y()
    partial(x, into(keep))
    qa.to_z()
    p4.to_x()
    p56.to_x()
    p0.pass_x()
    links.wait(far_in, at_x(xs), id_far)
    links.wait(sum_in, at_x(xr), id_sum)
    keep[...] += far_in[...].astype(F32) + sum_in[...].astype(F32)
    mine = pl.ds(pl.multiple_of(yh * 128, 128), 128)
    theirs = pl.ds(pl.multiple_of(oyh * 128, 128), 128)
    ypart_out[...] = keep[theirs, :].astype(BF)
    links.send(ypart_out, at_y, id_y, dst=ypart_in)
    qb.to_z()
    q1.pass_z()
    p0.finish()
    links.wait(ypart_in, at_y, id_y)
    lat[...] = (keep[mine, :] + ypart_in[...].astype(F32)).astype(BF)
    p0.done()

    def start_tile(n, carry):
        cols = pl.ds(pl.multiple_of(n * 256, 256), 256)
        total = dot(lat[...], w0b[:, :, :, :, cols].reshape(1024, 256))
        lift1[:, cols] = snake(total, a0_ref[:, cols]).astype(BF)
        return carry

    lax.fori_loop(0, 6, start_tile, 0)
    qa.pass_z()
    q1.finish()
    p4.pass_x()
    p56.pass_x()
    q1.done()

    def up1_tile(n, carry):
        cols = pl.ds(pl.multiple_of(n * 256, 256), 256)
        total = dot(lift1[...], w1b[:, :, :, :, cols].reshape(1536, 256))
        phase, part = lax.div(n, 3), lax.rem(n, 3)
        up1[:, phase, :, pl.ds(pl.multiple_of(part * 256, 256), 256)] = total.reshape(16, 8, 256)
        return carry

    lax.fori_loop(0, 6, up1_tile, 0)
    qb.pass_z()
    qa.finish()
    p4.finish()
    p56.finish()

    act_a1[pl.ds(0, 8 * PAD1), :] = jnp.zeros((8 * PAD1, 768), BF)
    act_a1[pl.ds(8 * (PAD1 + 32), 8 * PAD1), :] = jnp.zeros((8 * PAD1, 768), BF)
    act_b1[pl.ds(0, 8 * PAD1), :] = jnp.zeros((8 * PAD1, 768), BF)
    act_b1[pl.ds(8 * (PAD1 + 34), 8 * PAD1), :] = jnp.zeros((8 * PAD1, 768), BF)

    def act1_tile(n, carry):
        cols = pl.ds(pl.multiple_of(n * 256, 256), 256)
        act = snake(up1[:, :, :, cols].reshape(256, 256), a1_ref[:, cols])
        edge = jnp.zeros((8, 256), F32)
        act_a1[pl.ds(8 * PAD1, 256), cols] = act.astype(BF)
        act_b1[pl.ds(8 * PAD1, 272), cols] = jnp.concatenate([edge, act, edge], axis=0).astype(BF)
        return carry

    lax.fori_loop(0, 3, act1_tile, 0)
    qa.done()

    def conv1_tile(taps, n):
        cols = pl.ds(pl.multiple_of(n * 256, 256), 256)
        total = None
        for tap in taps:
            shift = 3 * (tap - 3)
            if shift % 2:
                window = act_b1[pl.ds(8 * (PAD1 + 1 + shift), 256), :]
            else:
                window = act_a1[pl.ds(8 * (PAD1 + shift), 256), :]
            term = dot(window, w23b[tap, :, :, :, :, cols].reshape(768, 256))
            total = term if total is None else total + term
        return cols, total

    def conv1_even(n, carry):
        cols, total = conv1_tile((0, 2, 4, 6), n)
        acc1[:, cols] = total
        return carry

    def conv1_odd(n, carry):
        cols, total = conv1_tile((1, 3, 5), n)
        sec1[:, cols] = snake(acc1[:, cols] + total, a1_ref[:, cols]).astype(BF)
        return carry

    lax.fori_loop(0, 3, conv1_even, 0)
    qb.finish()
    qb.done()
    lax.fori_loop(0, 3, conv1_odd, 0)

    def mix1_tile(n, carry):
        cols = pl.ds(pl.multiple_of(n * 256, 256), 256)
        total = dot(sec1[...], w23b[7, :, :, :, :, cols].reshape(768, 256))
        block = up1[:, :, :, cols].reshape(256, 256) + total
        lift2[:, cols] = snake(block, a2_ref[:, cols]).astype(BF)
        return carry

    lax.fori_loop(0, 3, mix1_tile, 0)
    p4.done()

    def up2_tile(n, carry):
        rows = pl.ds(pl.multiple_of(n * 64, 64), 64)
        total = dot(lift2[rows, :], w4b[...].reshape(768, 768))
        for phase in range(2):
            up2[pl.ds(n * 8, 8), phase] = total[:, phase * 384 : (phase + 1) * 384].reshape(8, 8, 384)
        return carry

    lax.fori_loop(0, 4, up2_tile, 0)

    act_a2[pl.ds(0, 8 * PAD2), :] = jnp.zeros((8 * PAD2, 384), BF)
    act_a2[pl.ds(8 * (PAD2 + 64), 8 * PAD2), :] = jnp.zeros((8 * PAD2, 384), BF)
    act_b2[pl.ds(0, 8 * PAD2), :] = jnp.zeros((8 * PAD2, 384), BF)
    act_b2[pl.ds(8 * (PAD2 + 66), 8 * PAD2), :] = jnp.zeros((8 * PAD2, 384), BF)

    def act2_tile(n, carry):
        cols = pl.ds(pl.multiple_of(n * 128, 128), 128)
        act = snake(up2[:, :, :, cols].reshape(512, 128), a3_ref[:, cols])
        edge = jnp.zeros((8, 128), F32)
        act_a2[pl.ds(8 * PAD2, 512), cols] = act.astype(BF)
        act_b2[pl.ds(8 * PAD2, 528), cols] = jnp.concatenate([edge, act, edge], axis=0).astype(BF)
        return carry

    lax.fori_loop(0, 3, act2_tile, 0)
    p56.done()

    def conv2_tile(n, carry):
        start = n * 128
        total = None
        for tap in range(7):
            shift = 9 * (tap - 3)
            if shift % 2:
                window = act_b2[pl.ds(pl.multiple_of(8 * (PAD2 + 1 + shift) + start, 16), 128), :]
            else:
                window = act_a2[pl.ds(pl.multiple_of(8 * (PAD2 + shift) + start, 16), 128), :]
            term = dot(window, w56b[tap // 4, tap % 4].reshape(384, 384))
            total = term if total is None else total + term
        second = snake(total, a3_ref[...]).astype(BF)
        block = up2[pl.ds(n * 8, 8)].reshape(128, 384) + dot(second, w56b[1, 3].reshape(384, 384))
        block2[pl.ds(pl.multiple_of(start, 128), 128), :] = block.astype(BF)
        return carry

    lax.fori_loop(0, 4, conv2_tile, 0)

    gap = lax.broadcasted_iota(jnp.int32, (64, 512), 1) - 8 * lax.broadcasted_iota(jnp.int32, (64, 512), 0)
    for owner in range(8):
        pick = jnp.concatenate(
            [jnp.where(gap == src_ref[owner * MOST + r], 1.0, 0.0).astype(BF) for r in range(MOST)], axis=0
        )
        outbuf[owner] = dot(pick, block2[...]).astype(BF)
    out_ids = [links.new() for _ in owners]
    here = pl.ds(pl.multiple_of(d * 128, 128), 128)
    for number, o in zip(out_ids, owners):
        links.send(outbuf.at[o], {"fsdp": f, "dp": o}, number, dst=out_ref.at[here])
    out_ref[here, :] = outbuf[d]
    for number in out_ids:
        links.wait(out_ref.at[here], sib, number)
    for copy in links.sent:
        copy.wait_send()


def body(codes, lengths, owner, codebook, w0, a0, w1, a1, w2, w3, a2, w4, a3, w5, w6):
    count = lengths.shape[0]
    dest = owner[:, 0]
    order = lax.iota(jnp.int32, count)
    earlier = (dest[None, :] == dest[:, None]) & (order[None, :] < order[:, None])
    rank = jnp.sum(earlier.astype(jnp.int32), axis=1)
    slot = dest * MOST + rank
    routed = slot[None, :] == lax.iota(jnp.int32, 8 * MOST)[:, None]
    src = jnp.max(jnp.where(routed, order[None, :], -8192), axis=1).astype(jnp.int32)
    frames = codes.reshape(9, count, SLAB).transpose(0, 2, 1)
    kept = lax.iota(jnp.int32, SLAB)[:, None] < lengths[None, :]
    frames = jnp.where(kept[None], frames, -1).reshape(9, SLAB * count)
    frames = jnp.pad(frames, ((0, 7), (0, 0)), constant_values=-1)
    w23 = jnp.concatenate([w2, w3[None]], axis=0)
    w56 = jnp.concatenate([w5, w6[None]], axis=0)
    vmem = pl.BlockSpec(memory_space=pltpu.VMEM)
    anywhere = pl.BlockSpec(memory_space=pl.ANY)
    V = pltpu.VMEM
    sems = 90
    return pl.pallas_call(
        kernel,
        out_shape=jax.ShapeDtypeStruct((1024, 384), BF),
        in_specs=[vmem, pl.BlockSpec(memory_space=pltpu.SMEM)] + [anywhere] * 6 + [vmem] * 4,
        out_specs=vmem,
        scratch_shapes=[
            V((4, 2, 16, 128), jnp.int32),
            V((9, 64, 1024), F32),
            V((64, 1536), F32),
            V((96, 384), F32),
            V((2, 48, 768), F32),
            V((48, 768), F32),
            V((4, 48, 384), F32),
            V((9, 128, 1024), BF),
            V((1152, 256), BF),
            V((256, 1024), BF),
            V((256, 1024), BF),
            V((256, 1024), BF),
            V((256, 1024), BF),
            V((256, 1024), BF),
            V((256, 1024), BF),
            V((256, 1024), F32),
            V((128, 1024), BF),
            V((128, 1024), BF),
            V((4, 2, 2, 64, 1536), BF),
            V((4, 2, 2, 96, 1536), BF),
            V((8, 4, 2, 2, 48, 768), BF),
            V((4, 2, 2, 48, 768), BF),
            V((2, 4, 4, 2, 48, 384), BF),
            V((128, 1024), BF),
            V((128, 1536), BF),
            V((16, 2, 8, 768), F32),
            V((8 * (2 * PAD1 + 32), 768), BF),
            V((8 * (2 * PAD1 + 34), 768), BF),
            V((256, 768), F32),
            V((256, 768), BF),
            V((256, 768), BF),
            V((32, 2, 8, 384), F32),
            V((8 * (2 * PAD2 + 64), 384), BF),
            V((8 * (2 * PAD2 + 66), 384), BF),
            V((512, 384), BF),
            V((512, 384), BF),
            V((8, 128, 384), BF),
            pltpu.SemaphoreType.DMA((sems,)),
            pltpu.SemaphoreType.DMA((sems,)),
            pltpu.SemaphoreType.DMA((6,)),
        ],
        compiler_params=pltpu.CompilerParams(
            collective_id=0, has_side_effects=True, vmem_limit_bytes=60 * 1024 * 1024
        ),
        cost_estimate=pl.CostEstimate(flops=7_400_000_000, bytes_accessed=8_000_000, transcendentals=0),
    )(frames, src, codebook, w0, w1, w23, w4, w56, a0[None], a1[None], a2[None], a3[None])


def solution(mesh):
    return jax.shard_map(
        body,
        mesh=mesh,
        in_specs=(
            P(None, ("fsdp", "dp")),
            P(("fsdp", "dp")),
            P(("fsdp", "dp"), None),
            P(None, "fsdp", None),
            P("fsdp", None),
            P(),
            P("fsdp", None),
            P(),
            P(None, "fsdp", None),
            P("fsdp", None),
            P(),
            P("fsdp", None),
            P(),
            P(None, "fsdp", None),
            P("fsdp", None),
        ),
        out_specs=P(("fsdp", "dp"), None),
        check_vma=False,
    )
```

```python
import jax
import jax.numpy as jnp
from jax import lax
from jax.experimental import pallas as pl
from jax.experimental.pallas import tpu as pltpu
from jax.sharding import PartitionSpec as P

SLAB = 16
MOST = 2
BF = jnp.bfloat16
F32 = jnp.float32
POLY = (
    9.869604311819561,
    -32.46967117891694,
    42.72719645855932,
    -30.101466599015037,
    13.05010051862992,
    -3.3565928630444257,
)
INV_PI = 0.3183098861837907
PAD1 = 8
PAD2 = 26


def snake(value, freq):
    turns = value * (freq * INV_PI)
    frac = turns - jnp.round(turns)
    u = frac * frac
    poly = jnp.full_like(u, POLY[-1])
    for coef in POLY[-2::-1]:
        poly = poly * u + coef
    return value + (poly * u) * (1.0 / freq)


def dot(left, right):
    return jnp.dot(left, right, preferred_element_type=F32)


class Links:
    def __init__(self, send_sems, recv_sems):
        self.send_sems, self.recv_sems, self.used, self.sent = send_sems, recv_sems, 0, []

    def new(self):
        self.used += 1
        return self.used - 1

    def copy(self, src, dst, dev, number):
        return pltpu.make_async_remote_copy(
            src_ref=src,
            dst_ref=dst,
            send_sem=self.send_sems.at[number],
            recv_sem=self.recv_sems.at[number],
            device_id=dev,
            device_id_type=pl.DeviceIdType.MESH,
        )

    def send(self, src, dev, number, dst=None):
        copy = self.copy(src, src if dst is None else dst, dev, number)
        copy.start()
        self.sent.append(copy)

    def wait(self, region, dev, number):
        self.copy(region, region, dev, number).wait_recv()


def kernel(
    codes_ref, lens_ref, owner_ref, cb_hbm, w0_hbm, a0_ref, w1_hbm, a1_ref, w2_hbm, w3_hbm, a2_ref, w4_hbm, a3_ref, w5_hbm, w6_hbm,
    out_ref,
    codes_all, cbf, w0f, w1f, wzf, whf, w4f, s56, table, onehot,
    fwd_out, fwd_in, far_out, far_in, sum_out, sum_in, keep, ypart_out, ypart_in,
    w0b, w1b, w23b, w4b, w56b,
    lat, lift1, up1, act_a1, act_b1, acc1, sec1, lift2, up2, act_a2, act_b2, sec2, block2, outbuf,
    send_sems, recv_sems, local_sems,
):
    f = lax.axis_index("fsdp")
    d = lax.axis_index("dp")
    x, yh, c = lax.div(f, 4), lax.rem(lax.div(f, 2), 2), lax.rem(f, 2)
    yl, z = lax.div(d, 4), lax.rem(d, 4)
    g = x * 2 + yh

    def dev(x_, yh_, yl_, z_, c_):
        return {"fsdp": (x_ * 2 + yh_) * 2 + c_, "dp": yl_ * 4 + z_}

    def plus(value, step):
        return lax.rem(value + step, 4)

    xp, xm, x2 = plus(x, 1), plus(x, 3), plus(x, 2)
    zp, zm, z2 = plus(z, 1), plus(z, 3), plus(z, 2)
    xs, xr = plus(x, 1 + 2 * c), plus(x, 3 + 2 * c)
    oyh = 1 - yh
    oyl = 1 - yl

    def at_x(xt):
        return dev(xt, yh, yl, z, c)

    def at_z(zt):
        return dev(x, yh, yl, zt, c)

    at_y = dev(x, oyh, oyl, z, c)
    at_b = dev(x, yh, oyl, z, c)
    sib = dev(x, yh, yl, z, 1 - c)
    links = Links(send_sems, recv_sems)
    local_count = [0]

    def load(src, dst):
        copy = pltpu.make_async_copy(src, dst, local_sems.at[local_count[0]])
        local_count[0] += 1
        copy.start()
        return copy

    zcols = pl.ds(pl.multiple_of(z * 384, 384), 384)
    ld_w1 = load(w1_hbm.at[:, zcols], w1f)
    ld_w0 = load(w0_hbm, w0f)
    ld_cb = load(cb_hbm, cbf)
    ld_wz = load(w2_hbm.at[z], wzf)
    ld_wh = load(w2_hbm.at[pl.ds(4, 3)], whf.at[pl.ds(0, 3)])
    ld_w3 = load(w3_hbm, whf.at[3])
    ld_w4 = load(w4_hbm, w4f)
    own24 = pl.ds(pl.multiple_of(c * 24, 8), 24)
    s56_own = s56.at[own24]
    own_last = (c == 1) & (z == 3)
    sib_last = (c == 0) & (z == 3)
    ld_56 = pltpu.make_async_copy(w6_hbm, s56_own, local_sems.at[7])

    @pl.when(own_last)
    def _():
        ld_56.start()

    @pl.when(jnp.logical_not(own_last))
    def _():
        pltpu.make_async_copy(w5_hbm.at[lax.rem(4 * c + z, 7)], s56_own, local_sems.at[7]).start()

    lane = lax.broadcasted_iota(jnp.int32, (9, 128), 1)
    room = jnp.zeros((9, 128), jnp.int32)
    for slab in range(8):
        room = jnp.where(lax.div(lane, SLAB) == slab, lens_ref[slab], room)
    codes_all[x, yh] = jnp.where(lax.rem(lane, SLAB) < room, codes_ref[...], -1)

    mates = []
    for step in range(4):
        if step:
            mates.append(at_x(plus(x, step)))
        mates.append(dev(plus(x, step), oyh, oyl, z, c))
    owners = [lax.rem(d + step, 8) for step in range(1, 8)]
    barrier = pltpu.get_barrier_semaphore()
    peers = mates + [sib] + [{"fsdp": f, "dp": o} for o in owners]
    for peer in peers:
        pl.semaphore_signal(barrier, inc=1, device_id=peer, device_id_type=pl.DeviceIdType.MESH)
    pl.semaphore_wait(barrier, len(peers))

    class Quarter:
        def __init__(self, block, row, full):
            self.block, self.row, self.full = block, row, full
            self.ids = [links.new() for _ in range(17)]

        def start(self):
            for number, place in zip(self.ids[:4], (at_x(xp), at_x(xm), at_x(x2), at_y)):
                links.send(self.block(z, x, yh), place, number)

        def x_in(self):
            for k, xt in enumerate((xm, xp, x2)):
                links.wait(self.block(z, xt, yh), at_x(xt), self.ids[k])
                links.send(self.block(z, xt, yh), at_y, self.ids[4 + k])
            links.send(self.row(z, yh), at_z(zp), self.ids[7])
            links.send(self.row(z, yh), at_z(zm), self.ids[8])

        def y_in(self):
            for k, xt in enumerate((x, xm, xp, x2)):
                links.wait(self.block(z, xt, oyh), at_y, self.ids[3 + k])
            links.send(self.row(z, oyh), at_z(zp), self.ids[9])
            links.send(self.row(z, oyh), at_z(zm), self.ids[10])
            links.send(self.full(z), sib, self.ids[13])

        def pass_own(self):
            links.wait(self.row(zm, yh), at_z(zm), self.ids[7])
            links.send(self.row(zm, yh), at_z(zp), self.ids[11])
            links.wait(self.row(zp, yh), at_z(zp), self.ids[8])

        def pass_other(self):
            links.wait(self.row(zp, oyh), at_z(zp), self.ids[10])
            links.send(self.row(zp, oyh), at_z(zm), self.ids[12])
            links.wait(self.row(zm, oyh), at_z(zm), self.ids[9])
            links.send(self.full(zp), sib, self.ids[14])
            links.send(self.full(zm), sib, self.ids[15])

        def finish(self):
            links.wait(self.row(z2, yh), at_z(zm), self.ids[11])
            links.wait(self.row(z2, oyh), at_z(zp), self.ids[12])
            links.send(self.full(z2), sib, self.ids[16])

        def done(self):
            for number, zt in zip(self.ids[13:], (z, zp, zm, z2)):
                links.wait(self.full(zt), sib, number)

    class Plain:
        def __init__(self, block, pair):
            self.block, self.pair = block, pair
            self.ids = [links.new() for _ in range(11)]

        def start(self):
            for number, place in zip(self.ids[:3], (at_y, at_x(xp), at_x(xm))):
                links.send(self.block(x, yh), place, number)

        def to_x(self):
            links.wait(self.block(x, oyh), at_y, self.ids[0])
            links.send(self.block(x, oyh), at_x(xp), self.ids[3])
            links.send(self.block(x, oyh), at_x(xm), self.ids[4])
            links.send(self.pair(x), sib, self.ids[7])

        def pass_own(self):
            links.wait(self.block(xm, yh), at_x(xm), self.ids[1])
            links.send(self.block(xm, yh), at_x(xp), self.ids[5])
            links.wait(self.block(xp, yh), at_x(xp), self.ids[2])

        def pass_other(self):
            links.wait(self.block(xp, oyh), at_x(xp), self.ids[4])
            links.send(self.block(xp, oyh), at_x(xm), self.ids[6])
            links.wait(self.block(xm, oyh), at_x(xm), self.ids[3])
            links.send(self.pair(xp), sib, self.ids[8])
            links.send(self.pair(xm), sib, self.ids[9])

        def finish(self):
            links.wait(self.block(x2, yh), at_x(xm), self.ids[5])
            links.wait(self.block(x2, oyh), at_x(xp), self.ids[6])
            links.send(self.pair(x2), sib, self.ids[10])

        def done(self):
            for number, xt in zip(self.ids[7:], (x, xp, xm, x2)):
                links.wait(self.pair(xt), sib, number)

    class Half:
        def __init__(self, block, pair, full):
            self.block, self.pair, self.full = block, pair, full
            self.ids = [links.new() for _ in range(13)]

        def start(self):
            links.send(self.block(oyl, x, yh), at_y, self.ids[0])
            links.send(self.block(yl, x, yh), at_x(xp), self.ids[1])
            links.send(self.block(yl, x, yh), at_x(xm), self.ids[2])

        def to_x(self):
            links.wait(self.block(yl, x, oyh), at_y, self.ids[0])
            links.send(self.block(yl, x, oyh), at_x(xp), self.ids[3])
            links.send(self.block(yl, x, oyh), at_x(xm), self.ids[4])
            links.send(self.block(yl, x, oyh), at_b, self.ids[7])

        def pass_own(self):
            links.wait(self.block(yl, xm, yh), at_x(xm), self.ids[1])
            links.send(self.block(yl, xm, yh), at_x(xp), self.ids[5])
            links.wait(self.block(yl, xp, yh), at_x(xp), self.ids[2])

        def pass_other(self):
            links.wait(self.block(yl, xp, oyh), at_x(xp), self.ids[4])
            links.send(self.block(yl, xp, oyh), at_x(xm), self.ids[6])
            links.wait(self.block(yl, xm, oyh), at_x(xm), self.ids[3])
            links.send(self.pair(yl, xp), at_b, self.ids[8])
            links.send(self.pair(yl, xm), at_b, self.ids[9])

        def finish(self):
            links.wait(self.block(yl, x2, yh), at_x(xm), self.ids[5])
            links.wait(self.block(yl, x2, oyh), at_x(xp), self.ids[6])
            links.send(self.pair(yl, x2), at_b, self.ids[10])
            links.send(self.full(yl), sib, self.ids[11])

        def b_in(self):
            links.wait(self.block(oyl, x, oyh), at_b, self.ids[7])
            for number, xt in zip(self.ids[8:11], (xp, xm, x2)):
                links.wait(self.pair(oyl, xt), at_b, number)
            links.send(self.full(oyl), sib, self.ids[12])

        def done(self):
            links.wait(self.full(yl), sib, self.ids[11])
            links.wait(self.full(oyl), sib, self.ids[12])

    def columns(zt):
        return pl.ds(pl.multiple_of(zt * 384, 384), 384)

    def pair_of_taps(t):
        return pl.ds(4 + 2 * t, 2)

    q1 = Quarter(
        lambda zt, xt, yt: w1b.at[xt, yt, c, :, columns(zt)],
        lambda zt, yt: w1b.at[:, yt, c, :, columns(zt)],
        lambda zt: w1b.at[:, :, c, :, columns(zt)],
    )
    qz = Quarter(
        lambda zt, xt, yt: w23b.at[zt, xt, yt, c],
        lambda zt, yt: w23b.at[zt, :, yt, c],
        lambda zt: w23b.at[zt, :, :, c],
    )
    q56 = Quarter(
        lambda zt, xt, yt: w56b.at[c, zt, xt, yt],
        lambda zt, yt: w56b.at[c, zt, :, yt],
        lambda zt: w56b.at[c, zt],
    )
    hh = Half(
        lambda t, xt, yt: w23b.at[pair_of_taps(t), xt, yt, c],
        lambda t, xt: w23b.at[pair_of_taps(t), xt, :, c],
        lambda t: w23b.at[pair_of_taps(t), :, :, c],
    )
    p0 = Plain(lambda xt, yt: w0b.at[xt, yt, c], lambda xt: w0b.at[xt, :, c])
    p4 = Plain(lambda xt, yt: w4b.at[xt, yt, c], lambda xt: w4b.at[xt, :, c])

    ld_w1.wait()
    w1b[x, yh, c, :, zcols] = w1f[...].astype(BF)
    q1.start()
    code_ids = [links.new() for _ in mates]
    for number, mate in zip(code_ids, mates):
        links.send(codes_all.at[x, yh], mate, number)
    ld_w0.wait()
    w0b[x, yh, c] = w0f[...].astype(BF)
    p0.start()

    ld_cb.wait()
    own64 = pl.ds(pl.multiple_of(c * 64, 64), 64)
    oth64 = pl.ds(pl.multiple_of((1 - c) * 64, 64), 64)
    for level in range(9):
        table[level, own64, :] = cbf[level].astype(BF)
    id_table = links.new()
    links.send(table.at[:, own64], sib, id_table)

    id_56 = links.new()
    to_56 = links.copy(w6_hbm, s56_own, sib, id_56)
    links.sent.append(to_56)

    @pl.when(sib_last)
    def _():
        to_56.start()

    @pl.when(jnp.logical_not(sib_last))
    def _():
        links.copy(w5_hbm.at[lax.rem(4 * (1 - c) + z, 7)], s56_own, sib, id_56).start()

    q1.x_in()
    ld_wz.wait()
    w23b[z, x, yh, c] = wzf[...].astype(BF)
    qz.start()

    for number, mate in zip(code_ids, mates):
        links.wait(codes_all.at[x, yh], mate, number)
    links.wait(table.at[:, oth64], sib, id_table)

    def partial(xt, put):
        place = lax.broadcasted_iota(jnp.int32, (128, 128), 0) + g * 128
        for yt in range(2):
            codes = codes_all[xt, yt]
            for level in range(9):
                hit = codes[level : level + 1, :] == place
                onehot[pl.ds(level * 128, 128), pl.ds(yt * 128, 128)] = jnp.where(hit, 1.0, 0.0).astype(BF)

        def tile(n, carry):
            cols = pl.ds(pl.multiple_of(n * 256, 256), 256)
            rows = table[:, :, cols].reshape(1152, 256)
            total = lax.dot_general(onehot[...], rows, (((0,), (0,)), ((), ())), preferred_element_type=F32)
            put(cols, total)
            return carry

        lax.fori_loop(0, 4, tile, 0)

    def into(ref):
        def put(cols, total):
            ref[:, cols] = total.astype(ref.dtype)

        return put

    id_fwd, id_far, id_sum, id_y = (links.new() for _ in range(4))
    partial(x2, into(fwd_out))
    links.send(fwd_out, at_x(xs), id_fwd, dst=fwd_in)
    partial(xr, into(far_out))
    links.send(far_out, at_x(xr), id_far, dst=far_in)
    q1.y_in()
    p0.to_x()
    qz.x_in()
    partial(xs, into(keep))
    links.wait(fwd_in, at_x(xr), id_fwd)
    sum_out[...] = (keep[...] + fwd_in[...].astype(F32)).astype(BF)
    links.send(sum_out, at_x(xs), id_sum, dst=sum_in)
    p0.pass_own()
    q1.pass_own()
    qz.y_in()
    ld_56.wait()
    links.wait(s56_own, sib, id_56)
    w56b[c, z, x, yh] = s56[...].astype(BF)
    q56.start()
    ld_wh.wait()
    ld_w3.wait()
    for k in range(4):
        w23b[4 + k, x, yh, c] = whf[k].astype(BF)
    hh.start()
    partial(x, into(keep))
    p0.pass_other()
    q1.pass_other()
    q56.x_in()
    ld_w4.wait()
    w4b[x, yh, c] = w4f[...].astype(BF)
    links.wait(far_in, at_x(xs), id_far)
    links.wait(sum_in, at_x(xr), id_sum)
    keep[...] += far_in[...].astype(F32) + sum_in[...].astype(F32)
    mine = pl.ds(pl.multiple_of(yh * 128, 128), 128)
    theirs = pl.ds(pl.multiple_of(oyh * 128, 128), 128)
    ypart_out[...] = keep[theirs, :].astype(BF)
    links.send(ypart_out, at_y, id_y, dst=ypart_in)
    p4.start()
    hh.to_x()
    qz.pass_own()
    q56.y_in()
    p0.finish()
    q1.finish()
    hh.pass_own()
    p4.to_x()
    links.wait(ypart_in, at_y, id_y)
    keep[mine, :] += ypart_in[...].astype(F32)
    row = lax.broadcasted_iota(jnp.int32, (128, 128), 0)
    place = lax.broadcasted_iota(jnp.int32, (128, 128), 1)
    order = jnp.where(place == lax.rem(row, 8) * SLAB + lax.div(row, 8), 1.0, 0.0).astype(BF)
    lat[...] = dot(order, keep[mine, :].astype(BF)).astype(BF)
    p0.done()

    def start_tile(n, carry):
        cols = pl.ds(pl.multiple_of(n * 256, 256), 256)
        total = dot(lat[...], w0b[:, :, :, :, cols].reshape(1024, 256))
        lift1[:, cols] = snake(total, a0_ref[cols].reshape(1, 256)).astype(BF)
        return carry

    lax.fori_loop(0, 6, start_tile, 0)
    qz.pass_other()
    hh.pass_other()
    q1.done()

    def up1_tile(n, carry):
        cols = pl.ds(pl.multiple_of(n * 256, 256), 256)
        total = dot(lift1[...], w1b[:, :, :, :, cols].reshape(1536, 256))
        phase, part = lax.div(n, 3), lax.rem(n, 3)
        up1[:, phase, :, pl.ds(pl.multiple_of(part * 256, 256), 256)] = total.reshape(16, 8, 256)
        return carry

    lax.fori_loop(0, 6, up1_tile, 0)
    p4.pass_own()
    q56.pass_own()
    hh.finish()
    p4.pass_other()

    act_a1[pl.ds(0, 8 * PAD1), :] = jnp.zeros((8 * PAD1, 768), BF)
    act_a1[pl.ds(8 * (PAD1 + 32), 8 * PAD1), :] = jnp.zeros((8 * PAD1, 768), BF)
    act_b1[pl.ds(0, 8 * PAD1), :] = jnp.zeros((8 * PAD1, 768), BF)
    act_b1[pl.ds(8 * (PAD1 + 34), 8 * PAD1), :] = jnp.zeros((8 * PAD1, 768), BF)

    def act1_tile(n, carry):
        cols = pl.ds(pl.multiple_of(n * 256, 256), 256)
        act = snake(up1[:, :, :, cols].reshape(256, 256), a1_ref[cols].reshape(1, 256))
        edge = jnp.zeros((8, 256), F32)
        act_a1[pl.ds(8 * PAD1, 256), cols] = act.astype(BF)
        act_b1[pl.ds(8 * PAD1, 272), cols] = jnp.concatenate([edge, act, edge], axis=0).astype(BF)
        return carry

    lax.fori_loop(0, 3, act1_tile, 0)
    qz.finish()
    hh.b_in()
    p4.finish()
    q56.pass_other()

    def conv1_tile(taps, n):
        cols = pl.ds(pl.multiple_of(n * 256, 256), 256)
        total = None
        for tap in taps:
            shift = 3 * (tap - 3)
            if shift % 2:
                window = act_b1[pl.ds(8 * (PAD1 + 1 + shift), 256), :]
            else:
                window = act_a1[pl.ds(8 * (PAD1 + shift), 256), :]
            term = dot(window, w23b[tap, :, :, :, :, cols].reshape(768, 256))
            total = term if total is None else total + term
        return cols, total

    def conv1_first(n, carry):
        cols, total = conv1_tile((0, 1, 2, 3), n)
        acc1[:, cols] = total
        return carry

    def conv1_rest(n, carry):
        cols, total = conv1_tile((4, 5, 6), n)
        sec1[:, cols] = snake(acc1[:, cols] + total, a1_ref[cols].reshape(1, 256)).astype(BF)
        return carry

    qz.done()
    lax.fori_loop(0, 3, conv1_first, 0)
    hh.done()
    lax.fori_loop(0, 3, conv1_rest, 0)

    def mix1_tile(n, carry):
        cols = pl.ds(pl.multiple_of(n * 256, 256), 256)
        total = dot(sec1[...], w23b[7, :, :, :, :, cols].reshape(768, 256))
        block = up1[:, :, :, cols].reshape(256, 256) + total
        lift2[:, cols] = snake(block, a2_ref[cols].reshape(1, 256)).astype(BF)
        return carry

    lax.fori_loop(0, 3, mix1_tile, 0)
    q56.finish()
    p4.done()

    def up2_tile(n, carry):
        rows = pl.ds(pl.multiple_of(n * 64, 64), 64)
        total = dot(lift2[rows, :], w4b[...].reshape(768, 768))
        for phase in range(2):
            up2[pl.ds(n * 8, 8), phase] = total[:, phase * 384 : (phase + 1) * 384].reshape(8, 8, 384)
        return carry

    lax.fori_loop(0, 4, up2_tile, 0)

    act_a2[pl.ds(0, 8 * PAD2), :] = jnp.zeros((8 * PAD2, 384), BF)
    act_a2[pl.ds(8 * (PAD2 + 64), 8 * PAD2), :] = jnp.zeros((8 * PAD2, 384), BF)
    act_b2[pl.ds(0, 8 * PAD2), :] = jnp.zeros((8 * PAD2, 384), BF)
    act_b2[pl.ds(8 * (PAD2 + 66), 8 * PAD2), :] = jnp.zeros((8 * PAD2, 384), BF)

    def act2_tile(n, carry):
        cols = pl.ds(pl.multiple_of(n * 128, 128), 128)
        act = snake(up2[:, :, :, cols].reshape(512, 128), a3_ref[cols].reshape(1, 128))
        edge = jnp.zeros((8, 128), F32)
        act_a2[pl.ds(8 * PAD2, 512), cols] = act.astype(BF)
        act_b2[pl.ds(8 * PAD2, 528), cols] = jnp.concatenate([edge, act, edge], axis=0).astype(BF)
        return carry

    lax.fori_loop(0, 3, act2_tile, 0)
    q56.done()

    def conv2_tile(n, carry):
        start = n * 128
        total = None
        for tap in range(7):
            shift = 9 * (tap - 3)
            if shift % 2:
                window = act_b2[pl.ds(pl.multiple_of(8 * (PAD2 + 1 + shift) + start, 16), 128), :]
            else:
                window = act_a2[pl.ds(pl.multiple_of(8 * (PAD2 + shift) + start, 16), 128), :]
            term = dot(window, w56b[tap // 4, tap % 4].reshape(384, 384))
            total = term if total is None else total + term
        second = snake(total, a3_ref[...].reshape(1, 384)).astype(BF)
        block = up2[pl.ds(n * 8, 8)].reshape(128, 384) + dot(second, w56b[1, 3].reshape(384, 384))
        block2[pl.ds(pl.multiple_of(start, 128), 128), :] = block.astype(BF)
        return carry

    lax.fori_loop(0, 4, conv2_tile, 0)

    dest = [owner_ref[slab, 0] for slab in range(8)]
    slots = []
    for slab in range(8):
        rank = jnp.int32(0)
        for before in range(slab):
            rank = rank + jnp.where(dest[before] == dest[slab], 1, 0)
        slots.append(dest[slab] * MOST + rank)
    lane = lax.broadcasted_iota(jnp.int32, (64, 512), 1)
    named = jnp.zeros((64, 512), jnp.int32)
    for slab in range(8):
        named = jnp.where(lax.rem(lane, 8) == slab, slots[slab], named)
    named = jnp.where(lax.div(lane, 8) == lax.broadcasted_iota(jnp.int32, (64, 512), 0), named, -1)
    for owner in range(8):
        pick = jnp.concatenate(
            [jnp.where(named == owner * MOST + r, 1.0, 0.0).astype(BF) for r in range(MOST)], axis=0
        )
        outbuf[owner] = dot(pick, block2[...]).astype(BF)
    out_ids = [links.new() for _ in owners]
    here = pl.ds(pl.multiple_of(d * 128, 128), 128)
    for number, o in zip(out_ids, owners):
        links.send(outbuf.at[o], {"fsdp": f, "dp": o}, number, dst=out_ref.at[here])
    out_ref[here, :] = outbuf[d]
    for number in out_ids:
        links.wait(out_ref.at[here], sib, number)
    for copy in links.sent:
        copy.wait_send()


def body(codes, lengths, owner, *rest):
    vmem = pl.BlockSpec(memory_space=pltpu.VMEM)
    smem = pl.BlockSpec(memory_space=pltpu.SMEM)
    hbm = pl.BlockSpec(memory_space=pl.ANY)
    V = pltpu.VMEM
    sems = 150
    return pl.pallas_call(
        kernel,
        out_shape=jax.ShapeDtypeStruct((1024, 384), BF),
        in_specs=[vmem, smem, smem, hbm, hbm, vmem, hbm, vmem, hbm, hbm, vmem, hbm, vmem, hbm, hbm],
        out_specs=vmem,
        scratch_shapes=[
            V((4, 2, 9, 128), jnp.int32),
            V((9, 64, 1024), F32),
            V((64, 1536), F32),
            V((96, 384), F32),
            V((48, 768), F32),
            V((4, 48, 768), F32),
            V((48, 768), F32),
            V((48, 384), F32),
            V((9, 128, 1024), BF),
            V((1152, 256), BF),
            V((256, 1024), BF),
            V((256, 1024), BF),
            V((256, 1024), BF),
            V((256, 1024), BF),
            V((256, 1024), BF),
            V((256, 1024), BF),
            V((256, 1024), F32),
            V((128, 1024), BF),
            V((128, 1024), BF),
            V((4, 2, 2, 64, 1536), BF),
            V((4, 2, 2, 96, 1536), BF),
            V((8, 4, 2, 2, 48, 768), BF),
            V((4, 2, 2, 48, 768), BF),
            V((2, 4, 4, 2, 48, 384), BF),
            V((128, 1024), BF),
            V((128, 1536), BF),
            V((16, 2, 8, 768), F32),
            V((8 * (2 * PAD1 + 32), 768), BF),
            V((8 * (2 * PAD1 + 34), 768), BF),
            V((256, 768), F32),
            V((256, 768), BF),
            V((256, 768), BF),
            V((32, 2, 8, 384), F32),
            V((8 * (2 * PAD2 + 64), 384), BF),
            V((8 * (2 * PAD2 + 66), 384), BF),
            V((512, 384), BF),
            V((512, 384), BF),
            V((8, 128, 384), BF),
            pltpu.SemaphoreType.DMA((sems,)),
            pltpu.SemaphoreType.DMA((sems,)),
            pltpu.SemaphoreType.DMA((8,)),
        ],
        compiler_params=pltpu.CompilerParams(
            collective_id=0, has_side_effects=True, vmem_limit_bytes=60 * 1024 * 1024
        ),
        cost_estimate=pl.CostEstimate(flops=7_400_000_000, bytes_accessed=8_000_000, transcendentals=0),
    )(codes, lengths, owner, *rest)


def solution(mesh):
    return jax.shard_map(
        body,
        mesh=mesh,
        in_specs=(
            P(None, ("fsdp", "dp")),
            P(("fsdp", "dp")),
            P(("fsdp", "dp"), None),
            P(None, "fsdp", None),
            P("fsdp", None),
            P(),
            P("fsdp", None),
            P(),
            P(None, "fsdp", None),
            P("fsdp", None),
            P(),
            P("fsdp", None),
            P(),
            P(None, "fsdp", None),
            P("fsdp", None),
        ),
        out_specs=P(("fsdp", "dp"), None),
        check_vma=False,
    )
```

```python
import jax
import jax.numpy as jnp
from jax import lax
from jax.experimental import pallas as pl
from jax.experimental.pallas import tpu as pltpu
from jax.sharding import PartitionSpec as P

SLAB = 16
MOST = 2
BF = jnp.bfloat16
F32 = jnp.float32
POLY = (
    9.869604311819561,
    -32.46967117891694,
    42.72719645855932,
    -30.101466599015037,
    13.05010051862992,
    -3.3565928630444257,
)
INV_PI = 0.3183098861837907
PAD1 = 8
PAD2 = 26


def snake(value, freq):
    turns = value * (freq * INV_PI)
    frac = turns - jnp.round(turns)
    u = frac * frac
    poly = jnp.full_like(u, POLY[-1])
    for coef in POLY[-2::-1]:
        poly = poly * u + coef
    return value + (poly * u) * (1.0 / freq)


def dot(left, right):
    return jnp.dot(left, right, preferred_element_type=F32)


class Links:
    def __init__(self, send_sems, recv_sems):
        self.send_sems, self.recv_sems, self.used, self.sent = send_sems, recv_sems, 0, []

    def new(self):
        self.used += 1
        return self.used - 1

    def copy(self, src, dst, dev, number):
        return pltpu.make_async_remote_copy(
            src_ref=src,
            dst_ref=dst,
            send_sem=self.send_sems.at[number],
            recv_sem=self.recv_sems.at[number],
            device_id=dev,
            device_id_type=pl.DeviceIdType.MESH,
        )

    def send(self, src, dev, number, dst=None):
        copy = self.copy(src, src if dst is None else dst, dev, number)
        copy.start()
        self.sent.append(copy)

    def wait(self, region, dev, number):
        self.copy(region, region, dev, number).wait_recv()


def kernel(
    codes_ref, lens_ref, owner_ref, cb_hbm, w0_hbm, a0_ref, w1_hbm, a1_ref, w2_hbm, w3_hbm, a2_ref, w4_hbm, a3_ref, w5_hbm, w6_hbm,
    out_ref,
    codes_all, cbf, w0f, w1f, wzf, whf, w4f, s56, table, onehot,
    fwd_out, fwd_in, far_out, far_in, sum_out, sum_in, keep, ypart_out, ypart_in,
    w0b, w1b, w23b, w4b, w56b,
    lat, lift1, up1, act_a1, act_b1, acc1, sec1, lift2, up2, act_a2, act_b2, pick, outbuf,
    send_sems, recv_sems, local_sems,
):
    f = lax.axis_index("fsdp")
    d = lax.axis_index("dp")
    x, yh, c = lax.div(f, 4), lax.rem(lax.div(f, 2), 2), lax.rem(f, 2)
    yl, z = lax.div(d, 4), lax.rem(d, 4)
    g = x * 2 + yh

    def dev(x_, yh_, yl_, z_, c_):
        return {"fsdp": (x_ * 2 + yh_) * 2 + c_, "dp": yl_ * 4 + z_}

    def plus(value, step):
        return lax.rem(value + step, 4)

    xp, xm, x2 = plus(x, 1), plus(x, 3), plus(x, 2)
    zp, zm, z2 = plus(z, 1), plus(z, 3), plus(z, 2)
    xs, xr = plus(x, 1 + 2 * c), plus(x, 3 + 2 * c)
    oyh = 1 - yh
    oyl = 1 - yl

    def at_x(xt):
        return dev(xt, yh, yl, z, c)

    def at_z(zt):
        return dev(x, yh, yl, zt, c)

    at_y = dev(x, oyh, oyl, z, c)
    at_b = dev(x, yh, oyl, z, c)
    sib = dev(x, yh, yl, z, 1 - c)
    links = Links(send_sems, recv_sems)
    local_count = [0]

    def load(src, dst):
        copy = pltpu.make_async_copy(src, dst, local_sems.at[local_count[0]])
        local_count[0] += 1
        copy.start()
        return copy

    zcols = pl.ds(pl.multiple_of(z * 384, 384), 384)
    ld_w1 = load(w1_hbm.at[:, zcols], w1f)
    ld_w0 = load(w0_hbm, w0f)
    ld_cb = load(cb_hbm, cbf)
    ld_wz = load(w2_hbm.at[z], wzf)
    ld_wh = load(w2_hbm.at[pl.ds(4, 3)], whf.at[pl.ds(0, 3)])
    ld_w3 = load(w3_hbm, whf.at[3])
    ld_w4 = load(w4_hbm, w4f)
    own24 = pl.ds(pl.multiple_of(c * 24, 8), 24)
    s56_own = s56.at[own24]
    own_last = (c == 1) & (z == 3)
    sib_last = (c == 0) & (z == 3)
    ld_56 = pltpu.make_async_copy(w6_hbm, s56_own, local_sems.at[7])

    @pl.when(own_last)
    def _():
        ld_56.start()

    @pl.when(jnp.logical_not(own_last))
    def _():
        pltpu.make_async_copy(w5_hbm.at[lax.rem(4 * c + z, 7)], s56_own, local_sems.at[7]).start()

    lane = lax.broadcasted_iota(jnp.int32, (9, 128), 1)
    room = jnp.zeros((9, 128), jnp.int32)
    for slab in range(8):
        room = jnp.where(lax.div(lane, SLAB) == slab, lens_ref[slab], room)
    codes_all[x, yh] = jnp.where(lax.rem(lane, SLAB) < room, codes_ref[...], -1)

    mates = []
    for step in range(4):
        if step:
            mates.append(at_x(plus(x, step)))
        mates.append(dev(plus(x, step), oyh, oyl, z, c))
    owners = [lax.rem(d + step, 8) for step in range(1, 8)]
    barrier = pltpu.get_barrier_semaphore()
    peers = mates + [sib] + [{"fsdp": f, "dp": o} for o in owners]
    for peer in peers:
        pl.semaphore_signal(barrier, inc=1, device_id=peer, device_id_type=pl.DeviceIdType.MESH)
    pl.semaphore_wait(barrier, len(peers))

    class Quarter:
        def __init__(self, block, row, full):
            self.block, self.row, self.full = block, row, full
            self.ids = [links.new() for _ in range(17)]

        def start(self):
            for number, place in zip(self.ids[:4], (at_x(xp), at_x(xm), at_x(x2), at_y)):
                links.send(self.block(z, x, yh), place, number)

        def x_in(self):
            for k, xt in enumerate((xm, xp, x2)):
                links.wait(self.block(z, xt, yh), at_x(xt), self.ids[k])
                links.send(self.block(z, xt, yh), at_y, self.ids[4 + k])
            links.send(self.row(z, yh), at_z(zp), self.ids[7])
            links.send(self.row(z, yh), at_z(zm), self.ids[8])

        def y_in(self):
            for k, xt in enumerate((x, xm, xp, x2)):
                links.wait(self.block(z, xt, oyh), at_y, self.ids[3 + k])
            links.send(self.row(z, oyh), at_z(zp), self.ids[9])
            links.send(self.row(z, oyh), at_z(zm), self.ids[10])
            links.send(self.full(z), sib, self.ids[13])

        def pass_own(self):
            links.wait(self.row(zm, yh), at_z(zm), self.ids[7])
            links.send(self.row(zm, yh), at_z(zp), self.ids[11])
            links.wait(self.row(zp, yh), at_z(zp), self.ids[8])

        def pass_other(self):
            links.wait(self.row(zp, oyh), at_z(zp), self.ids[10])
            links.send(self.row(zp, oyh), at_z(zm), self.ids[12])
            links.wait(self.row(zm, oyh), at_z(zm), self.ids[9])
            links.send(self.full(zp), sib, self.ids[14])
            links.send(self.full(zm), sib, self.ids[15])

        def finish(self):
            links.wait(self.row(z2, yh), at_z(zm), self.ids[11])
            links.wait(self.row(z2, oyh), at_z(zp), self.ids[12])
            links.send(self.full(z2), sib, self.ids[16])

        def done(self):
            for number, zt in zip(self.ids[13:], (z, zp, zm, z2)):
                links.wait(self.full(zt), sib, number)

    class Plain:
        def __init__(self, block, pair):
            self.block, self.pair = block, pair
            self.ids = [links.new() for _ in range(11)]

        def start(self):
            for number, place in zip(self.ids[:3], (at_y, at_x(xp), at_x(xm))):
                links.send(self.block(x, yh), place, number)

        def to_x(self):
            links.wait(self.block(x, oyh), at_y, self.ids[0])
            links.send(self.block(x, oyh), at_x(xp), self.ids[3])
            links.send(self.block(x, oyh), at_x(xm), self.ids[4])
            links.send(self.pair(x), sib, self.ids[7])

        def pass_own(self):
            links.wait(self.block(xm, yh), at_x(xm), self.ids[1])
            links.send(self.block(xm, yh), at_x(xp), self.ids[5])
            links.wait(self.block(xp, yh), at_x(xp), self.ids[2])

        def pass_other(self):
            links.wait(self.block(xp, oyh), at_x(xp), self.ids[4])
            links.send(self.block(xp, oyh), at_x(xm), self.ids[6])
            links.wait(self.block(xm, oyh), at_x(xm), self.ids[3])
            links.send(self.pair(xp), sib, self.ids[8])
            links.send(self.pair(xm), sib, self.ids[9])

        def finish(self):
            links.wait(self.block(x2, yh), at_x(xm), self.ids[5])
            links.wait(self.block(x2, oyh), at_x(xp), self.ids[6])
            links.send(self.pair(x2), sib, self.ids[10])

        def done(self):
            for number, xt in zip(self.ids[7:], (x, xp, xm, x2)):
                links.wait(self.pair(xt), sib, number)

    class Half:
        def __init__(self, block, pair, full):
            self.block, self.pair, self.full = block, pair, full
            self.ids = [links.new() for _ in range(13)]

        def start(self):
            links.send(self.block(oyl, x, yh), at_y, self.ids[0])
            links.send(self.block(yl, x, yh), at_x(xp), self.ids[1])
            links.send(self.block(yl, x, yh), at_x(xm), self.ids[2])

        def to_x(self):
            links.wait(self.block(yl, x, oyh), at_y, self.ids[0])
            links.send(self.block(yl, x, oyh), at_x(xp), self.ids[3])
            links.send(self.block(yl, x, oyh), at_x(xm), self.ids[4])
            links.send(self.block(yl, x, oyh), at_b, self.ids[7])

        def pass_own(self):
            links.wait(self.block(yl, xm, yh), at_x(xm), self.ids[1])
            links.send(self.block(yl, xm, yh), at_x(xp), self.ids[5])
            links.wait(self.block(yl, xp, yh), at_x(xp), self.ids[2])

        def pass_other(self):
            links.wait(self.block(yl, xp, oyh), at_x(xp), self.ids[4])
            links.send(self.block(yl, xp, oyh), at_x(xm), self.ids[6])
            links.wait(self.block(yl, xm, oyh), at_x(xm), self.ids[3])
            links.send(self.pair(yl, xp), at_b, self.ids[8])
            links.send(self.pair(yl, xm), at_b, self.ids[9])

        def finish(self):
            links.wait(self.block(yl, x2, yh), at_x(xm), self.ids[5])
            links.wait(self.block(yl, x2, oyh), at_x(xp), self.ids[6])
            links.send(self.pair(yl, x2), at_b, self.ids[10])
            links.send(self.full(yl), sib, self.ids[11])

        def b_in(self):
            links.wait(self.block(oyl, x, oyh), at_b, self.ids[7])
            for number, xt in zip(self.ids[8:11], (xp, xm, x2)):
                links.wait(self.pair(oyl, xt), at_b, number)
            links.send(self.full(oyl), sib, self.ids[12])

        def done(self):
            links.wait(self.full(yl), sib, self.ids[11])
            links.wait(self.full(oyl), sib, self.ids[12])

    def columns(zt):
        return pl.ds(pl.multiple_of(zt * 384, 384), 384)

    def pair_of_taps(t):
        return pl.ds(4 + 2 * t, 2)

    q1 = Quarter(
        lambda zt, xt, yt: w1b.at[xt, yt, c, :, columns(zt)],
        lambda zt, yt: w1b.at[:, yt, c, :, columns(zt)],
        lambda zt: w1b.at[:, :, c, :, columns(zt)],
    )
    qz = Quarter(
        lambda zt, xt, yt: w23b.at[zt, xt, yt, c],
        lambda zt, yt: w23b.at[zt, :, yt, c],
        lambda zt: w23b.at[zt, :, :, c],
    )
    q56 = Quarter(
        lambda zt, xt, yt: w56b.at[c, zt, xt, yt],
        lambda zt, yt: w56b.at[c, zt, :, yt],
        lambda zt: w56b.at[c, zt],
    )
    hh = Half(
        lambda t, xt, yt: w23b.at[pair_of_taps(t), xt, yt, c],
        lambda t, xt: w23b.at[pair_of_taps(t), xt, :, c],
        lambda t: w23b.at[pair_of_taps(t), :, :, c],
    )
    p0 = Plain(lambda xt, yt: w0b.at[xt, yt, c], lambda xt: w0b.at[xt, :, c])
    p4 = Plain(lambda xt, yt: w4b.at[xt, yt, c], lambda xt: w4b.at[xt, :, c])

    code_ids = [links.new() for _ in mates]
    for number, mate in zip(code_ids, mates):
        links.send(codes_all.at[x, yh], mate, number)

    id_56 = links.new()
    to_56 = links.copy(w6_hbm, s56_own, sib, id_56)
    links.sent.append(to_56)

    @pl.when(sib_last)
    def _():
        to_56.start()

    @pl.when(jnp.logical_not(sib_last))
    def _():
        links.copy(w5_hbm.at[lax.rem(4 * (1 - c) + z, 7)], s56_own, sib, id_56).start()

    ld_w1.wait()
    w1b[x, yh, c, :, zcols] = w1f[...].astype(BF)
    q1.start()
    ld_wz.wait()
    w23b[z, x, yh, c] = wzf[...].astype(BF)
    qz.start()
    ld_56.wait()
    links.wait(s56_own, sib, id_56)
    w56b[c, z, x, yh] = s56[...].astype(BF)
    q56.start()

    ld_cb.wait()
    own64 = pl.ds(pl.multiple_of(c * 64, 64), 64)
    oth64 = pl.ds(pl.multiple_of((1 - c) * 64, 64), 64)
    for level in range(9):
        table[level, own64, :] = cbf[level].astype(BF)
    id_table = links.new()
    links.send(table.at[:, own64], sib, id_table)
    q1.x_in()
    ld_wh.wait()
    ld_w3.wait()
    for k in range(4):
        w23b[4 + k, x, yh, c] = whf[k].astype(BF)
    hh.start()

    for number, mate in zip(code_ids, mates):
        links.wait(codes_all.at[x, yh], mate, number)
    links.wait(table.at[:, oth64], sib, id_table)

    def partial(xt, put):
        place = lax.broadcasted_iota(jnp.int32, (128, 128), 0) + g * 128
        for yt in range(2):
            codes = codes_all[xt, yt]
            for level in range(9):
                hit = codes[level : level + 1, :] == place
                onehot[pl.ds(level * 128, 128), pl.ds(yt * 128, 128)] = jnp.where(hit, 1.0, 0.0).astype(BF)

        def tile(n, carry):
            cols = pl.ds(pl.multiple_of(n * 256, 256), 256)
            rows = table[:, :, cols].reshape(1152, 256)
            total = lax.dot_general(onehot[...], rows, (((0,), (0,)), ((), ())), preferred_element_type=F32)
            put(cols, total)
            return carry

        lax.fori_loop(0, 4, tile, 0)

    def into(ref):
        def put(cols, total):
            ref[:, cols] = total.astype(ref.dtype)

        return put

    id_fwd, id_far, id_sum, id_y = (links.new() for _ in range(4))
    partial(x2, into(fwd_out))
    links.send(fwd_out, at_x(xs), id_fwd, dst=fwd_in)
    qz.x_in()
    partial(xr, into(far_out))
    links.send(far_out, at_x(xr), id_far, dst=far_in)
    q56.x_in()
    hh.to_x()
    q1.y_in()
    ld_w0.wait()
    w0b[x, yh, c] = w0f[...].astype(BF)
    p0.start()
    partial(xs, into(keep))
    q1.pass_own()
    qz.y_in()
    hh.pass_own()
    q56.y_in()
    q1.pass_other()
    hh.pass_other()
    links.wait(fwd_in, at_x(xr), id_fwd)
    sum_out[...] = (keep[...] + fwd_in[...].astype(F32)).astype(BF)
    links.send(sum_out, at_x(xs), id_sum, dst=sum_in)
    partial(x, into(keep))
    p0.to_x()
    p0.pass_own()
    hh.finish()
    ld_w4.wait()
    w4b[x, yh, c] = w4f[...].astype(BF)
    q1.finish()
    qz.pass_own()
    links.wait(far_in, at_x(xs), id_far)
    links.wait(sum_in, at_x(xr), id_sum)
    keep[...] += far_in[...].astype(F32) + sum_in[...].astype(F32)
    mine = pl.ds(pl.multiple_of(yh * 128, 128), 128)
    theirs = pl.ds(pl.multiple_of(oyh * 128, 128), 128)
    ypart_out[...] = keep[theirs, :].astype(BF)
    links.send(ypart_out, at_y, id_y, dst=ypart_in)
    p0.pass_other()
    p4.start()
    qz.pass_other()
    links.wait(ypart_in, at_y, id_y)
    keep[mine, :] += ypart_in[...].astype(F32)
    row = lax.broadcasted_iota(jnp.int32, (128, 128), 0)
    place = lax.broadcasted_iota(jnp.int32, (128, 128), 1)
    order = jnp.where(place == lax.rem(row, 8) * SLAB + lax.div(row, 8), 1.0, 0.0).astype(BF)
    lat[...] = dot(order, keep[mine, :].astype(BF)).astype(BF)
    p0.finish()
    p4.to_x()
    hh.b_in()
    p0.done()

    def start_tile(n, carry):
        cols = pl.ds(pl.multiple_of(n * 256, 256), 256)
        total = dot(lat[...], w0b[:, :, :, :, cols].reshape(1024, 256))
        lift1[:, cols] = snake(total, a0_ref[cols].reshape(1, 256)).astype(BF)
        return carry

    lax.fori_loop(0, 6, start_tile, 0)
    q56.pass_own()
    q1.done()

    def up1_tile(n, carry):
        cols = pl.ds(pl.multiple_of(n * 256, 256), 256)
        total = dot(lift1[...], w1b[:, :, :, :, cols].reshape(1536, 256))
        phase, part = lax.div(n, 3), lax.rem(n, 3)
        up1[:, phase, :, pl.ds(pl.multiple_of(part * 256, 256), 256)] = total.reshape(16, 8, 256)
        return carry

    lax.fori_loop(0, 6, up1_tile, 0)
    p4.pass_own()
    p4.pass_other()

    act_a1[pl.ds(0, 8 * PAD1), :] = jnp.zeros((8 * PAD1, 768), BF)
    act_a1[pl.ds(8 * (PAD1 + 32), 8 * PAD1), :] = jnp.zeros((8 * PAD1, 768), BF)
    act_b1[pl.ds(0, 8 * PAD1), :] = jnp.zeros((8 * PAD1, 768), BF)
    act_b1[pl.ds(8 * (PAD1 + 34), 8 * PAD1), :] = jnp.zeros((8 * PAD1, 768), BF)

    def act1_tile(n, carry):
        cols = pl.ds(pl.multiple_of(n * 256, 256), 256)
        act = snake(up1[:, :, :, cols].reshape(256, 256), a1_ref[cols].reshape(1, 256))
        edge = jnp.zeros((8, 256), F32)
        act_a1[pl.ds(8 * PAD1, 256), cols] = act.astype(BF)
        act_b1[pl.ds(8 * PAD1, 272), cols] = jnp.concatenate([edge, act, edge], axis=0).astype(BF)
        return carry

    lax.fori_loop(0, 3, act1_tile, 0)
    qz.finish()
    q56.pass_other()
    p4.finish()

    def conv1_tile(taps, n):
        cols = pl.ds(pl.multiple_of(n * 256, 256), 256)
        total = None
        for tap in taps:
            shift = 3 * (tap - 3)
            if shift % 2:
                window = act_b1[pl.ds(8 * (PAD1 + 1 + shift), 256), :]
            else:
                window = act_a1[pl.ds(8 * (PAD1 + shift), 256), :]
            term = dot(window, w23b[tap, :, :, :, :, cols].reshape(768, 256))
            total = term if total is None else total + term
        return cols, total

    def conv1_first(n, carry):
        cols, total = conv1_tile((0, 1, 2, 3), n)
        acc1[:, cols] = total
        return carry

    def conv1_rest(n, carry):
        cols, total = conv1_tile((4, 5, 6), n)
        sec1[:, cols] = snake(acc1[:, cols] + total, a1_ref[cols].reshape(1, 256)).astype(BF)
        return carry

    qz.done()
    lax.fori_loop(0, 3, conv1_first, 0)
    hh.done()
    lax.fori_loop(0, 3, conv1_rest, 0)

    def mix1_tile(n, carry):
        cols = pl.ds(pl.multiple_of(n * 256, 256), 256)
        total = dot(sec1[...], w23b[7, :, :, :, :, cols].reshape(768, 256))
        block = up1[:, :, :, cols].reshape(256, 256) + total
        lift2[:, cols] = snake(block, a2_ref[cols].reshape(1, 256)).astype(BF)
        return carry

    lax.fori_loop(0, 3, mix1_tile, 0)
    q56.finish()
    p4.done()

    def up2_tile(n, carry):
        rows = pl.ds(pl.multiple_of(n * 64, 64), 64)
        total = dot(lift2[rows, :], w4b[...].reshape(768, 768))
        for phase in range(2):
            up2[pl.ds(n * 8, 8), phase] = total[:, phase * 384 : (phase + 1) * 384].reshape(8, 8, 384)
        return carry

    lax.fori_loop(0, 4, up2_tile, 0)

    act_a2[pl.ds(0, 8 * PAD2), :] = jnp.zeros((8 * PAD2, 384), BF)
    act_a2[pl.ds(8 * (PAD2 + 64), 8 * PAD2), :] = jnp.zeros((8 * PAD2, 384), BF)
    act_b2[pl.ds(0, 8 * PAD2), :] = jnp.zeros((8 * PAD2, 384), BF)
    act_b2[pl.ds(8 * (PAD2 + 66), 8 * PAD2), :] = jnp.zeros((8 * PAD2, 384), BF)

    def act2_tile(n, carry):
        cols = pl.ds(pl.multiple_of(n * 128, 128), 128)
        act = snake(up2[:, :, :, cols].reshape(512, 128), a3_ref[cols].reshape(1, 128))
        edge = jnp.zeros((8, 128), F32)
        act_a2[pl.ds(8 * PAD2, 512), cols] = act.astype(BF)
        act_b2[pl.ds(8 * PAD2, 528), cols] = jnp.concatenate([edge, act, edge], axis=0).astype(BF)
        return carry

    lax.fori_loop(0, 3, act2_tile, 0)

    dest = [owner_ref[slab] for slab in range(8)]
    lane = lax.broadcasted_iota(jnp.int32, (16, 128), 1)
    named = jnp.zeros((16, 128), jnp.int32)
    for slab in range(8):
        rank = jnp.int32(0)
        for before in range(slab):
            rank = rank + jnp.where(dest[before] == dest[slab], 1, 0)
        named = jnp.where(lax.rem(lane, 8) == slab, dest[slab] * MOST + rank, named)
    named = jnp.where(lax.div(lane, 8) == lax.broadcasted_iota(jnp.int32, (16, 128), 0), named, -1)
    for slot in range(8 * MOST):
        pick[pl.ds(slot * 16, 16), :] = jnp.where(named == slot, 1.0, 0.0).astype(BF)
    q56.done()
    out_base = links.used

    def out_copy(n, k):
        frames = pl.ds(pl.multiple_of(n * 16, 16), 16)
        return links.copy(
            outbuf.at[n, owners[k]], out_ref.at[d, :, frames], {"fsdp": f, "dp": owners[k]}, out_base + n * 7 + k
        )

    def conv2_tile(n, carry):
        start = n * 128
        total = None
        for tap in range(7):
            shift = 9 * (tap - 3)
            if shift % 2:
                window = act_b2[pl.ds(pl.multiple_of(8 * (PAD2 + 1 + shift) + start, 16), 128), :]
            else:
                window = act_a2[pl.ds(pl.multiple_of(8 * (PAD2 + shift) + start, 16), 128), :]
            term = dot(window, w56b[tap // 4, tap % 4].reshape(384, 384))
            total = term if total is None else total + term
        second = snake(total, a3_ref[...].reshape(1, 384)).astype(BF)
        block = up2[pl.ds(n * 8, 8)].reshape(128, 384) + dot(second, w56b[1, 3].reshape(384, 384))
        slots = dot(pick[...], block.astype(BF)).astype(BF)
        outbuf[n] = slots.reshape(8, MOST, 16, 384)
        for k in range(7):
            out_copy(n, k).start()
        out_ref[d, :, pl.ds(pl.multiple_of(n * 16, 16), 16)] = outbuf[n, d]
        return carry

    lax.fori_loop(0, 4, conv2_tile, 0)

    def out_wait(n, carry):
        for k in range(7):
            out_copy(n, k).wait()
        return carry

    lax.fori_loop(0, 4, out_wait, 0)
    for copy in links.sent:
        copy.wait_send()


def body(codes, lengths, owner, *rest):
    vmem = pl.BlockSpec(memory_space=pltpu.VMEM)
    smem = pl.BlockSpec(memory_space=pltpu.SMEM)
    hbm = pl.BlockSpec(memory_space=pl.ANY)
    V = pltpu.VMEM
    sems = 170
    return pl.pallas_call(
        kernel,
        out_shape=jax.ShapeDtypeStruct((8, MOST, 64, 384), BF),
        in_specs=[vmem, smem, smem, hbm, hbm, vmem, hbm, vmem, hbm, hbm, vmem, hbm, vmem, hbm, hbm],
        out_specs=vmem,
        scratch_shapes=[
            V((4, 2, 9, 128), jnp.int32),
            V((9, 64, 1024), F32),
            V((64, 1536), F32),
            V((96, 384), F32),
            V((48, 768), F32),
            V((4, 48, 768), F32),
            V((48, 768), F32),
            V((48, 384), F32),
            V((9, 128, 1024), BF),
            V((1152, 256), BF),
            V((256, 1024), BF),
            V((256, 1024), BF),
            V((256, 1024), BF),
            V((256, 1024), BF),
            V((256, 1024), BF),
            V((256, 1024), BF),
            V((256, 1024), F32),
            V((128, 1024), BF),
            V((128, 1024), BF),
            V((4, 2, 2, 64, 1536), BF),
            V((4, 2, 2, 96, 1536), BF),
            V((8, 4, 2, 2, 48, 768), BF),
            V((4, 2, 2, 48, 768), BF),
            V((2, 4, 4, 2, 48, 384), BF),
            V((128, 1024), BF),
            V((128, 1536), BF),
            V((16, 2, 8, 768), F32),
            V((8 * (2 * PAD1 + 32), 768), BF),
            V((8 * (2 * PAD1 + 34), 768), BF),
            V((256, 768), F32),
            V((256, 768), BF),
            V((256, 768), BF),
            V((32, 2, 8, 384), F32),
            V((8 * (2 * PAD2 + 64), 384), BF),
            V((8 * (2 * PAD2 + 66), 384), BF),
            V((256, 128), BF),
            V((4, 8, MOST, 16, 384), BF),
            pltpu.SemaphoreType.DMA((sems,)),
            pltpu.SemaphoreType.DMA((sems,)),
            pltpu.SemaphoreType.DMA((8,)),
        ],
        compiler_params=pltpu.CompilerParams(
            collective_id=0, has_side_effects=True, vmem_limit_bytes=60 * 1024 * 1024
        ),
        cost_estimate=pl.CostEstimate(flops=7_400_000_000, bytes_accessed=8_000_000, transcendentals=0),
    )(codes, lengths, owner.reshape(8), *rest).reshape(1024, 384)


def solution(mesh):
    return jax.shard_map(
        body,
        mesh=mesh,
        in_specs=(
            P(None, ("fsdp", "dp")),
            P(("fsdp", "dp")),
            P(("fsdp", "dp"), None),
            P(None, "fsdp", None),
            P("fsdp", None),
            P(),
            P("fsdp", None),
            P(),
            P(None, "fsdp", None),
            P("fsdp", None),
            P(),
            P("fsdp", None),
            P(),
            P(None, "fsdp", None),
            P("fsdp", None),
        ),
        out_specs=P(("fsdp", "dp"), None),
        check_vma=False,
    )
```

```python
import jax
import jax.numpy as jnp
from jax import lax
from jax.experimental import pallas as pl
from jax.experimental.pallas import tpu as pltpu
from jax.sharding import PartitionSpec as P

SLAB = 16
MOST = 2
BF = jnp.bfloat16
F32 = jnp.float32
POLY = (
    9.869604311819561,
    -32.46967117891694,
    42.72719645855932,
    -30.101466599015037,
    13.05010051862992,
    -3.3565928630444257,
)
INV_PI = 0.3183098861837907
PAD1 = 8
PAD2 = 26


def snake(value, freq):
    turns = value * (freq * INV_PI)
    frac = turns - jnp.round(turns)
    u = frac * frac
    poly = jnp.full_like(u, POLY[-1])
    for coef in POLY[-2::-1]:
        poly = poly * u + coef
    return value + (poly * u) * (1.0 / freq)


def dot(left, right):
    return jnp.dot(left, right, preferred_element_type=F32)


class Links:
    def __init__(self, send_sems, recv_sems):
        self.send_sems, self.recv_sems, self.used, self.sent = send_sems, recv_sems, 0, []

    def new(self):
        self.used += 1
        return self.used - 1

    def copy(self, src, dst, dev, number):
        return pltpu.make_async_remote_copy(
            src_ref=src,
            dst_ref=dst,
            send_sem=self.send_sems.at[number],
            recv_sem=self.recv_sems.at[number],
            device_id=dev,
            device_id_type=pl.DeviceIdType.MESH,
        )

    def send(self, src, dev, number, dst=None):
        copy = self.copy(src, src if dst is None else dst, dev, number)
        copy.start()
        self.sent.append(copy)

    def wait(self, region, dev, number):
        self.copy(region, region, dev, number).wait_recv()


def kernel(
    codes_ref, lens_ref, owner_ref, cb_hbm, w0_hbm, a0_ref, w1_hbm, a1_ref, w2_hbm, w3_hbm, a2_ref, w4_hbm, a3_ref, w5_hbm, w6_hbm,
    out_ref,
    codes_all, cbf, w0f, w1f, wzf, whf, w4f, s56, table, onehot,
    fwd_out, fwd_in, far_out, far_in, sum_out, sum_in, keep, ypart_out, ypart_in,
    w0b, w1b, w23b, w4b, w56b,
    lat, lift1, up1, act_a1, act_b1, acc1, sec1, lift2, up2, act_a2, act_b2, pick, outbuf,
    send_sems, recv_sems, local_sems,
):
    f = lax.axis_index("fsdp")
    d = lax.axis_index("dp")
    x, yh, c = lax.div(f, 4), lax.rem(lax.div(f, 2), 2), lax.rem(f, 2)
    yl, z = lax.div(d, 4), lax.rem(d, 4)
    g = x * 2 + yh

    def dev(x_, yh_, yl_, z_, c_):
        return {"fsdp": (x_ * 2 + yh_) * 2 + c_, "dp": yl_ * 4 + z_}

    def plus(value, step):
        return lax.rem(value + step, 4)

    xp, xm, x2 = plus(x, 1), plus(x, 3), plus(x, 2)
    zp, zm, z2 = plus(z, 1), plus(z, 3), plus(z, 2)
    xs, xr = plus(x, 1 + 2 * c), plus(x, 3 + 2 * c)
    oyh = 1 - yh
    oyl = 1 - yl

    def at_x(xt):
        return dev(xt, yh, yl, z, c)

    def at_z(zt):
        return dev(x, yh, yl, zt, c)

    at_y = dev(x, oyh, oyl, z, c)
    at_b = dev(x, yh, oyl, z, c)
    sib = dev(x, yh, yl, z, 1 - c)
    links = Links(send_sems, recv_sems)
    local_count = [0]

    def load(src, dst):
        copy = pltpu.make_async_copy(src, dst, local_sems.at[local_count[0]])
        local_count[0] += 1
        copy.start()
        return copy

    zcols = pl.ds(pl.multiple_of(z * 384, 384), 384)
    ld_w1 = load(w1_hbm.at[:, zcols], w1f)
    ld_w0 = load(w0_hbm, w0f)
    ld_cb = load(cb_hbm, cbf)
    ld_wz = load(w2_hbm.at[z], wzf)
    ld_wh = load(w2_hbm.at[pl.ds(4, 3)], whf.at[pl.ds(0, 3)])
    ld_w3 = load(w3_hbm, whf.at[3])
    ld_w4 = load(w4_hbm, w4f)
    own24 = pl.ds(pl.multiple_of(c * 24, 8), 24)
    s56_own = s56.at[own24]
    own_last = (c == 1) & (z == 3)
    sib_last = (c == 0) & (z == 3)
    ld_56 = pltpu.make_async_copy(w6_hbm, s56_own, local_sems.at[7])

    @pl.when(own_last)
    def _():
        ld_56.start()

    @pl.when(jnp.logical_not(own_last))
    def _():
        pltpu.make_async_copy(w5_hbm.at[lax.rem(4 * c + z, 7)], s56_own, local_sems.at[7]).start()

    lane = lax.broadcasted_iota(jnp.int32, (9, 128), 1)
    room = jnp.zeros((9, 128), jnp.int32)
    for slab in range(8):
        room = jnp.where(lax.div(lane, SLAB) == slab, lens_ref[slab], room)
    codes_all[x, yh] = jnp.where(lax.rem(lane, SLAB) < room, codes_ref[...], -1)

    mates = []
    for step in range(4):
        if step:
            mates.append(at_x(plus(x, step)))
        mates.append(dev(plus(x, step), oyh, oyl, z, c))
    owners = [lax.rem(d + step, 8) for step in range(1, 8)]
    barrier = pltpu.get_barrier_semaphore()
    peers = mates + [sib] + [{"fsdp": f, "dp": o} for o in owners]
    for peer in peers:
        pl.semaphore_signal(barrier, inc=1, device_id=peer, device_id_type=pl.DeviceIdType.MESH)
    pl.semaphore_wait(barrier, len(peers))

    class Quarter:
        def __init__(self, block, row, full):
            self.block, self.row, self.full = block, row, full
            self.ids = [links.new() for _ in range(17)]

        def start(self):
            for number, place in zip(self.ids[:4], (at_x(xp), at_x(xm), at_x(x2), at_y)):
                links.send(self.block(z, x, yh), place, number)

        def x_in(self):
            for k, xt in enumerate((xm, xp, x2)):
                links.wait(self.block(z, xt, yh), at_x(xt), self.ids[k])
                links.send(self.block(z, xt, yh), at_y, self.ids[4 + k])
            links.send(self.row(z, yh), at_z(zp), self.ids[7])
            links.send(self.row(z, yh), at_z(zm), self.ids[8])

        def y_in(self):
            for k, xt in enumerate((x, xm, xp, x2)):
                links.wait(self.block(z, xt, oyh), at_y, self.ids[3 + k])
            links.send(self.row(z, oyh), at_z(zp), self.ids[9])
            links.send(self.row(z, oyh), at_z(zm), self.ids[10])
            links.send(self.full(z), sib, self.ids[13])

        def pass_own(self):
            links.wait(self.row(zm, yh), at_z(zm), self.ids[7])
            links.send(self.row(zm, yh), at_z(zp), self.ids[11])
            links.wait(self.row(zp, yh), at_z(zp), self.ids[8])

        def pass_other(self):
            links.wait(self.row(zp, oyh), at_z(zp), self.ids[10])
            links.send(self.row(zp, oyh), at_z(zm), self.ids[12])
            links.wait(self.row(zm, oyh), at_z(zm), self.ids[9])
            links.send(self.full(zp), sib, self.ids[14])
            links.send(self.full(zm), sib, self.ids[15])

        def finish(self):
            links.wait(self.row(z2, yh), at_z(zm), self.ids[11])
            links.wait(self.row(z2, oyh), at_z(zp), self.ids[12])
            links.send(self.full(z2), sib, self.ids[16])

        def done(self):
            for number, zt in zip(self.ids[13:], (z, zp, zm, z2)):
                links.wait(self.full(zt), sib, number)

    class Plain:
        def __init__(self, block, pair):
            self.block, self.pair = block, pair
            self.ids = [links.new() for _ in range(11)]

        def start(self):
            for number, place in zip(self.ids[:3], (at_y, at_x(xp), at_x(xm))):
                links.send(self.block(x, yh), place, number)

        def to_x(self):
            links.wait(self.block(x, oyh), at_y, self.ids[0])
            links.send(self.block(x, oyh), at_x(xp), self.ids[3])
            links.send(self.block(x, oyh), at_x(xm), self.ids[4])
            links.send(self.pair(x), sib, self.ids[7])

        def pass_own(self):
            links.wait(self.block(xm, yh), at_x(xm), self.ids[1])
            links.send(self.block(xm, yh), at_x(xp), self.ids[5])
            links.wait(self.block(xp, yh), at_x(xp), self.ids[2])

        def pass_other(self):
            links.wait(self.block(xp, oyh), at_x(xp), self.ids[4])
            links.send(self.block(xp, oyh), at_x(xm), self.ids[6])
            links.wait(self.block(xm, oyh), at_x(xm), self.ids[3])
            links.send(self.pair(xp), sib, self.ids[8])
            links.send(self.pair(xm), sib, self.ids[9])

        def finish(self):
            links.wait(self.block(x2, yh), at_x(xm), self.ids[5])
            links.wait(self.block(x2, oyh), at_x(xp), self.ids[6])
            links.send(self.pair(x2), sib, self.ids[10])

        def done(self):
            for number, xt in zip(self.ids[7:], (x, xp, xm, x2)):
                links.wait(self.pair(xt), sib, number)

    class Half:
        def __init__(self, block, pair, full):
            self.block, self.pair, self.full = block, pair, full
            self.ids = [links.new() for _ in range(13)]

        def start(self):
            links.send(self.block(oyl, x, yh), at_y, self.ids[0])
            links.send(self.block(yl, x, yh), at_x(xp), self.ids[1])
            links.send(self.block(yl, x, yh), at_x(xm), self.ids[2])

        def to_x(self):
            links.wait(self.block(yl, x, oyh), at_y, self.ids[0])
            links.send(self.block(yl, x, oyh), at_x(xp), self.ids[3])
            links.send(self.block(yl, x, oyh), at_x(xm), self.ids[4])
            links.send(self.block(yl, x, oyh), at_b, self.ids[7])

        def pass_own(self):
            links.wait(self.block(yl, xm, yh), at_x(xm), self.ids[1])
            links.send(self.block(yl, xm, yh), at_x(xp), self.ids[5])
            links.wait(self.block(yl, xp, yh), at_x(xp), self.ids[2])

        def pass_other(self):
            links.wait(self.block(yl, xp, oyh), at_x(xp), self.ids[4])
            links.send(self.block(yl, xp, oyh), at_x(xm), self.ids[6])
            links.wait(self.block(yl, xm, oyh), at_x(xm), self.ids[3])
            links.send(self.pair(yl, xp), at_b, self.ids[8])
            links.send(self.pair(yl, xm), at_b, self.ids[9])

        def finish(self):
            links.wait(self.block(yl, x2, yh), at_x(xm), self.ids[5])
            links.wait(self.block(yl, x2, oyh), at_x(xp), self.ids[6])
            links.send(self.pair(yl, x2), at_b, self.ids[10])
            links.send(self.full(yl), sib, self.ids[11])

        def b_in(self):
            links.wait(self.block(oyl, x, oyh), at_b, self.ids[7])
            for number, xt in zip(self.ids[8:11], (xp, xm, x2)):
                links.wait(self.pair(oyl, xt), at_b, number)
            links.send(self.full(oyl), sib, self.ids[12])

        def done(self):
            links.wait(self.full(yl), sib, self.ids[11])
            links.wait(self.full(oyl), sib, self.ids[12])

    def columns(zt):
        return pl.ds(pl.multiple_of(zt * 384, 384), 384)

    def pair_of_taps(t):
        return pl.ds(4 + 2 * t, 2)

    q1 = Quarter(
        lambda zt, xt, yt: w1b.at[xt, yt, c, :, columns(zt)],
        lambda zt, yt: w1b.at[:, yt, c, :, columns(zt)],
        lambda zt: w1b.at[:, :, c, :, columns(zt)],
    )
    qz = Quarter(
        lambda zt, xt, yt: w23b.at[zt, xt, yt, c],
        lambda zt, yt: w23b.at[zt, :, yt, c],
        lambda zt: w23b.at[zt, :, :, c],
    )
    q56 = Quarter(
        lambda zt, xt, yt: w56b.at[c, zt, xt, yt],
        lambda zt, yt: w56b.at[c, zt, :, yt],
        lambda zt: w56b.at[c, zt],
    )
    hh = Half(
        lambda t, xt, yt: w23b.at[pair_of_taps(t), xt, yt, c],
        lambda t, xt: w23b.at[pair_of_taps(t), xt, :, c],
        lambda t: w23b.at[pair_of_taps(t), :, :, c],
    )
    p0 = Plain(lambda xt, yt: w0b.at[xt, yt, c], lambda xt: w0b.at[xt, :, c])
    p4 = Plain(lambda xt, yt: w4b.at[xt, yt, c], lambda xt: w4b.at[xt, :, c])

    code_ids = [links.new() for _ in mates]
    for number, mate in zip(code_ids, mates):
        links.send(codes_all.at[x, yh], mate, number)

    id_56 = links.new()
    to_56 = links.copy(w6_hbm, s56_own, sib, id_56)
    links.sent.append(to_56)

    @pl.when(sib_last)
    def _():
        to_56.start()

    @pl.when(jnp.logical_not(sib_last))
    def _():
        links.copy(w5_hbm.at[lax.rem(4 * (1 - c) + z, 7)], s56_own, sib, id_56).start()

    ld_w1.wait()
    w1b[x, yh, c, :, zcols] = w1f[...].astype(BF)
    q1.start()
    ld_wz.wait()
    w23b[z, x, yh, c] = wzf[...].astype(BF)
    qz.start()
    ld_56.wait()
    links.wait(s56_own, sib, id_56)
    w56b[c, z, x, yh] = s56[...].astype(BF)
    q56.start()

    ld_cb.wait()
    own64 = pl.ds(pl.multiple_of(c * 64, 64), 64)
    oth64 = pl.ds(pl.multiple_of((1 - c) * 64, 64), 64)
    for level in range(9):
        table[level, own64, :] = cbf[level].astype(BF)
    id_table = links.new()
    links.send(table.at[:, own64], sib, id_table)
    q1.x_in()
    ld_wh.wait()
    ld_w3.wait()
    for k in range(4):
        w23b[4 + k, x, yh, c] = whf[k].astype(BF)
    hh.start()

    for number, mate in zip(code_ids, mates):
        links.wait(codes_all.at[x, yh], mate, number)
    links.wait(table.at[:, oth64], sib, id_table)

    def partial(xt, put):
        place = lax.broadcasted_iota(jnp.int32, (128, 128), 0) + g * 128
        for yt in range(2):
            codes = codes_all[xt, yt]
            for level in range(9):
                hit = codes[level : level + 1, :] == place
                onehot[pl.ds(yt * 128, 128), pl.ds(level * 128, 128)] = jnp.where(hit, 1.0, 0.0).T.astype(BF)

        def tile(n, carry):
            cols = pl.ds(pl.multiple_of(n * 256, 256), 256)
            rows = table[:, :, cols].reshape(1152, 256)
            total = dot(onehot[...], rows)
            put(cols, total)
            return carry

        lax.fori_loop(0, 4, tile, 0)

    def into(ref):
        def put(cols, total):
            ref[:, cols] = total.astype(ref.dtype)

        return put

    id_fwd, id_far, id_sum, id_y = (links.new() for _ in range(4))
    partial(x2, into(fwd_out))
    links.send(fwd_out, at_x(xs), id_fwd, dst=fwd_in)
    qz.x_in()
    partial(xr, into(far_out))
    links.send(far_out, at_x(xr), id_far, dst=far_in)
    q56.x_in()
    hh.to_x()
    q1.y_in()
    partial(xs, into(keep))
    q1.pass_own()
    qz.y_in()
    links.wait(fwd_in, at_x(xr), id_fwd)
    sum_out[...] = (keep[...] + fwd_in[...].astype(F32)).astype(BF)
    links.send(sum_out, at_x(xs), id_sum, dst=sum_in)
    hh.pass_own()
    q56.y_in()
    q1.pass_other()
    hh.pass_other()
    ld_w0.wait()
    w0b[x, yh, c] = w0f[...].astype(BF)
    p0.start()
    partial(x, into(keep))
    p0.to_x()
    p0.pass_own()
    hh.finish()
    ld_w4.wait()
    w4b[x, yh, c] = w4f[...].astype(BF)
    q1.finish()
    qz.pass_own()
    links.wait(far_in, at_x(xs), id_far)
    links.wait(sum_in, at_x(xr), id_sum)
    keep[...] += far_in[...].astype(F32) + sum_in[...].astype(F32)
    mine = pl.ds(pl.multiple_of(yh * 128, 128), 128)
    theirs = pl.ds(pl.multiple_of(oyh * 128, 128), 128)
    ypart_out[...] = keep[theirs, :].astype(BF)
    links.send(ypart_out, at_y, id_y, dst=ypart_in)
    p0.pass_other()
    p4.start()
    qz.pass_other()
    links.wait(ypart_in, at_y, id_y)
    keep[mine, :] += ypart_in[...].astype(F32)
    row = lax.broadcasted_iota(jnp.int32, (128, 128), 0)
    place = lax.broadcasted_iota(jnp.int32, (128, 128), 1)
    order = jnp.where(place == lax.rem(row, 8) * SLAB + lax.div(row, 8), 1.0, 0.0).astype(BF)
    lat[...] = dot(order, keep[mine, :].astype(BF)).astype(BF)
    p0.finish()
    p4.to_x()
    p0.done()

    def start_tile(n, carry):
        cols = pl.ds(pl.multiple_of(n * 256, 256), 256)
        total = dot(lat[...], w0b[:, :, :, :, cols].reshape(1024, 256))
        lift1[:, cols] = snake(total, a0_ref[cols].reshape(1, 256)).astype(BF)
        return carry

    lax.fori_loop(0, 6, start_tile, 0)
    q56.pass_own()
    q1.done()

    def up1_tile(n, carry):
        cols = pl.ds(pl.multiple_of(n * 256, 256), 256)
        total = dot(lift1[...], w1b[:, :, :, :, cols].reshape(1536, 256))
        phase, part = lax.div(n, 3), lax.rem(n, 3)
        up1[:, phase, :, pl.ds(pl.multiple_of(part * 256, 256), 256)] = total.reshape(16, 8, 256)
        return carry

    lax.fori_loop(0, 6, up1_tile, 0)
    hh.b_in()
    p4.pass_own()
    p4.pass_other()

    act_a1[pl.ds(0, 8 * PAD1), :] = jnp.zeros((8 * PAD1, 768), BF)
    act_a1[pl.ds(8 * (PAD1 + 32), 8 * PAD1), :] = jnp.zeros((8 * PAD1, 768), BF)
    act_b1[pl.ds(0, 8 * PAD1), :] = jnp.zeros((8 * PAD1, 768), BF)
    act_b1[pl.ds(8 * (PAD1 + 34), 8 * PAD1), :] = jnp.zeros((8 * PAD1, 768), BF)

    def act1_tile(n, carry):
        cols = pl.ds(pl.multiple_of(n * 256, 256), 256)
        act = snake(up1[:, :, :, cols].reshape(256, 256), a1_ref[cols].reshape(1, 256))
        edge = jnp.zeros((8, 256), F32)
        act_a1[pl.ds(8 * PAD1, 256), cols] = act.astype(BF)
        act_b1[pl.ds(8 * PAD1, 272), cols] = jnp.concatenate([edge, act, edge], axis=0).astype(BF)
        return carry

    lax.fori_loop(0, 3, act1_tile, 0)
    qz.finish()
    q56.pass_other()
    p4.finish()

    def conv1_tile(taps, n):
        cols = pl.ds(pl.multiple_of(n * 256, 256), 256)
        total = None
        for tap in taps:
            shift = 3 * (tap - 3)
            if shift % 2:
                window = act_b1[pl.ds(8 * (PAD1 + 1 + shift), 256), :]
            else:
                window = act_a1[pl.ds(8 * (PAD1 + shift), 256), :]
            term = dot(window, w23b[tap, :, :, :, :, cols].reshape(768, 256))
            total = term if total is None else total + term
        return cols, total

    def conv1_first(n, carry):
        cols, total = conv1_tile((0, 1, 2, 3), n)
        acc1[:, cols] = total
        return carry

    def conv1_rest(n, carry):
        cols, total = conv1_tile((4, 5, 6), n)
        sec1[:, cols] = snake(acc1[:, cols] + total, a1_ref[cols].reshape(1, 256)).astype(BF)
        return carry

    qz.done()
    lax.fori_loop(0, 3, conv1_first, 0)
    hh.done()
    lax.fori_loop(0, 3, conv1_rest, 0)

    def mix1_tile(n, carry):
        cols = pl.ds(pl.multiple_of(n * 256, 256), 256)
        total = dot(sec1[...], w23b[7, :, :, :, :, cols].reshape(768, 256))
        block = up1[:, :, :, cols].reshape(256, 256) + total
        lift2[:, cols] = snake(block, a2_ref[cols].reshape(1, 256)).astype(BF)
        return carry

    lax.fori_loop(0, 3, mix1_tile, 0)
    q56.finish()
    p4.done()

    def up2_tile(n, carry):
        rows = pl.ds(pl.multiple_of(n * 128, 128), 128)
        total = dot(lift2[rows, :], w4b[...].reshape(768, 768))
        for phase in range(2):
            up2[pl.ds(n * 16, 16), phase] = total[:, phase * 384 : (phase + 1) * 384].reshape(16, 8, 384)
        return carry

    lax.fori_loop(0, 2, up2_tile, 0)

    act_a2[pl.ds(0, 8 * PAD2), :] = jnp.zeros((8 * PAD2, 384), BF)
    act_a2[pl.ds(8 * (PAD2 + 64), 8 * PAD2), :] = jnp.zeros((8 * PAD2, 384), BF)
    act_b2[pl.ds(0, 8 * PAD2), :] = jnp.zeros((8 * PAD2, 384), BF)
    act_b2[pl.ds(8 * (PAD2 + 66), 8 * PAD2), :] = jnp.zeros((8 * PAD2, 384), BF)

    def act2_tile(n, carry):
        cols = pl.ds(pl.multiple_of(n * 128, 128), 128)
        act = snake(up2[:, :, :, cols].reshape(512, 128), a3_ref[cols].reshape(1, 128))
        edge = jnp.zeros((8, 128), F32)
        act_a2[pl.ds(8 * PAD2, 512), cols] = act.astype(BF)
        act_b2[pl.ds(8 * PAD2, 528), cols] = jnp.concatenate([edge, act, edge], axis=0).astype(BF)
        return carry

    lax.fori_loop(0, 3, act2_tile, 0)

    dest = [owner_ref[slab] for slab in range(8)]
    lane = lax.broadcasted_iota(jnp.int32, (32, 256), 1)
    named = jnp.zeros((32, 256), jnp.int32)
    for slab in range(8):
        rank = jnp.int32(0)
        for before in range(slab):
            rank = rank + jnp.where(dest[before] == dest[slab], 1, 0)
        named = jnp.where(lax.rem(lane, 8) == slab, dest[slab] * MOST + rank, named)
    named = jnp.where(lax.div(lane, 8) == lax.broadcasted_iota(jnp.int32, (32, 256), 0), named, -1)
    for slot in range(8 * MOST):
        pick[pl.ds(slot * 32, 32), :] = jnp.where(named == slot, 1.0, 0.0).astype(BF)
    q56.done()
    out_base = links.used

    def out_copy(n, k):
        frames = pl.ds(pl.multiple_of(n * 32, 32), 32)
        return links.copy(
            outbuf.at[n, owners[k]], out_ref.at[d, :, frames], {"fsdp": f, "dp": owners[k]}, out_base + n * 7 + k
        )

    def own_copy(n):
        frames = pl.ds(pl.multiple_of(n * 32, 32), 32)
        return pltpu.make_async_copy(outbuf.at[n, d], out_ref.at[d, :, frames], local_sems.at[8 + n])

    def conv2_tile(n, carry):
        start = n * 256
        total = None
        for tap in range(7):
            shift = 9 * (tap - 3)
            if shift % 2:
                window = act_b2[pl.ds(pl.multiple_of(8 * (PAD2 + 1 + shift) + start, 16), 256), :]
            else:
                window = act_a2[pl.ds(pl.multiple_of(8 * (PAD2 + shift) + start, 16), 256), :]
            term = dot(window, w56b[tap // 4, tap % 4].reshape(384, 384))
            total = term if total is None else total + term
        second = snake(total, a3_ref[...].reshape(1, 384)).astype(BF)
        block = up2[pl.ds(n * 16, 16)].reshape(256, 384) + dot(second, w56b[1, 3].reshape(384, 384))
        slots = dot(pick[...], block.astype(BF)).astype(BF)
        outbuf[n] = slots.reshape(8, MOST, 32, 384)
        for k in range(7):
            out_copy(n, k).start()
        own_copy(n).start()
        return carry

    lax.fori_loop(0, 2, conv2_tile, 0)

    def out_wait(n, carry):
        for k in range(7):
            out_copy(n, k).wait()
        own_copy(n).wait()
        return carry

    lax.fori_loop(0, 2, out_wait, 0)
    for copy in links.sent:
        copy.wait_send()


def body(codes, lengths, owner, *rest):
    vmem = pl.BlockSpec(memory_space=pltpu.VMEM)
    smem = pl.BlockSpec(memory_space=pltpu.SMEM)
    hbm = pl.BlockSpec(memory_space=pl.ANY)
    V = pltpu.VMEM
    sems = 170
    return pl.pallas_call(
        kernel,
        out_shape=jax.ShapeDtypeStruct((8, MOST, 64, 384), BF),
        in_specs=[vmem, smem, smem, hbm, hbm, vmem, hbm, vmem, hbm, hbm, vmem, hbm, vmem, hbm, hbm],
        out_specs=hbm,
        scratch_shapes=[
            V((4, 2, 9, 128), jnp.int32),
            V((9, 64, 1024), F32),
            V((64, 1536), F32),
            V((96, 384), F32),
            V((48, 768), F32),
            V((4, 48, 768), F32),
            V((48, 768), F32),
            V((48, 384), F32),
            V((9, 128, 1024), BF),
            V((256, 1152), BF),
            V((256, 1024), BF),
            V((256, 1024), BF),
            V((256, 1024), BF),
            V((256, 1024), BF),
            V((256, 1024), BF),
            V((256, 1024), BF),
            V((256, 1024), F32),
            V((128, 1024), BF),
            V((128, 1024), BF),
            V((4, 2, 2, 64, 1536), BF),
            V((4, 2, 2, 96, 1536), BF),
            V((8, 4, 2, 2, 48, 768), BF),
            V((4, 2, 2, 48, 768), BF),
            V((2, 4, 4, 2, 48, 384), BF),
            V((128, 1024), BF),
            V((128, 1536), BF),
            V((16, 2, 8, 768), F32),
            V((8 * (2 * PAD1 + 32), 768), BF),
            V((8 * (2 * PAD1 + 34), 768), BF),
            V((256, 768), F32),
            V((256, 768), BF),
            V((256, 768), BF),
            V((32, 2, 8, 384), F32),
            V((8 * (2 * PAD2 + 64), 384), BF),
            V((8 * (2 * PAD2 + 66), 384), BF),
            V((512, 256), BF),
            V((2, 8, MOST, 32, 384), BF),
            pltpu.SemaphoreType.DMA((sems,)),
            pltpu.SemaphoreType.DMA((sems,)),
            pltpu.SemaphoreType.DMA((10,)),
        ],
        compiler_params=pltpu.CompilerParams(
            collective_id=0, has_side_effects=True, vmem_limit_bytes=60 * 1024 * 1024
        ),
        cost_estimate=pl.CostEstimate(flops=7_400_000_000, bytes_accessed=8_000_000, transcendentals=0),
    )(codes, lengths, owner.reshape(8), *rest).reshape(1024, 384)


def solution(mesh):
    return jax.shard_map(
        body,
        mesh=mesh,
        in_specs=(
            P(None, ("fsdp", "dp")),
            P(("fsdp", "dp")),
            P(("fsdp", "dp"), None),
            P(None, "fsdp", None),
            P("fsdp", None),
            P(),
            P("fsdp", None),
            P(),
            P(None, "fsdp", None),
            P("fsdp", None),
            P(),
            P("fsdp", None),
            P(),
            P(None, "fsdp", None),
            P("fsdp", None),
        ),
        out_specs=P(("fsdp", "dp"), None),
        check_vma=False,
    )
```
